32 devices in a mesh: tm: 4 (over y, x), height: 4 (over z), width: 2 (over core).
Axes of the slice: x: 2, y: 2, z: 4, core: 2. Of those that a mesh axis runs over, the one named last changes fastest.
Arguments:
- video: bfloat16 [64, 64, 32, 256], P('tm', 'height', 'width'), may hold values from -12 to 12
- w_space: bfloat16 [3, 3, 256, 256], replicated, may hold values from -0.125 to 0.125
- w_time: bfloat16 [3, 256, 256], replicated, may hold values from -0.21875 to 0.21875
- norm_gain: float32 [256], replicated, may hold values from 0.1 to 1.9
- norm_bias: float32 [256], replicated, may hold values from -1 to 1
- w_qkv: bfloat16 [256, 768], replicated, may hold values from -64 to 64
- w_out: bfloat16 [256, 256], replicated, may hold values from -0.375 to 0.375
Outputs:
- block_out: bfloat16 [64, 64, 32, 256], P('tm', 'height', 'width')
The draws below stay inside these ranges and needn't reach their ends.
All inputs are finite; a program needn't handle non-finite values.
Results may differ from the reference program's by a relative error of at most 0.012.
Values may be sent and summed in bfloat16 or wider, within the bound.
A program may use at most 128 MiB of HBM per device.

```python
import math
import jax
import jax.numpy as jnp
from jax import lax

C = 256
HEADS = 8
GROUPS = 32
FRAMES = 64
HEIGHT = 64
WIDTH = 32


def draw_video(key, part):
    frame_pos = jnp.arange(FRAMES).astype(jnp.float32) / max(FRAMES - 1, 1)
    row_pos = jnp.arange(HEIGHT).astype(jnp.float32) / max(HEIGHT - 1, 1)
    col_pos = jnp.arange(WIDTH).astype(jnp.float32) / max(WIDTH - 1, 1)
    factor = jnp.sqrt((1.0 + 2.0 * frame_pos)[:, None, None] * (1.0 + 2.0 * row_pos)[None, :, None] * (1.0 + 2.0 * col_pos)[None, None, :])
    noise = jax.random.normal(jax.random.fold_in(key, 14), (FRAMES, HEIGHT, WIDTH, C), jnp.float32)
    return jnp.clip(noise * factor[:, :, :, None], -12.0, 12.0).astype(jnp.bfloat16)


def draw_w_qkv(key, part):
    base = jax.random.normal(jax.random.fold_in(key, 21), (C, 3 * C), jnp.float32) / jnp.sqrt(float(C))
    base = jnp.clip(base, -6.0 / jnp.sqrt(float(C)), 6.0 / jnp.sqrt(float(C)))
    return jnp.clip(base, -64.0, 64.0).astype(jnp.bfloat16)


def gaussian(rng, shape, deviation, limit, held_as=jnp.bfloat16):
    drawn = deviation * jax.random.normal(rng, shape, jnp.float32)
    return jnp.clip(drawn, min=-limit, max=limit).astype(held_as)


def setup_inputs(seed: int = 0) -> dict:
    seeds = jax.random.split(jax.random.key(seed), 8)
    return {
        "video": draw_video(jax.random.fold_in(seeds[7], 71), 0),
        "w_space": gaussian(seeds[1], (3, 3, C, C), (9 * C) ** -0.5, 0.125),
        "w_time": gaussian(seeds[2], (3, C, C), (3 * C) ** -0.5, 0.21875),
        "norm_gain": jnp.clip(1.0 + 0.18 * jax.random.normal(seeds[3], (C,), jnp.float32), 0.1, 1.9),
        "norm_bias": jnp.clip(jax.random.uniform(seeds[4], (C,), jnp.float32, -1.0, 1.0), -1.0, 1.0),
        "w_qkv": draw_w_qkv(jax.random.fold_in(seeds[7], 71), 0),
        "w_out": gaussian(seeds[6], (C, C), C ** -0.5, 0.375),
    }


def space_frame(frame, w_space):
    rows, cols, channels = frame.shape
    padded = jnp.pad(frame, ((1, 1), (1, 1), (0, 0)))
    running = jnp.zeros((rows * cols, channels), jnp.float32)
    for row_step in range(3):
        for col_step in range(3):
            window_piece = padded[row_step:row_step + rows, col_step:col_step + cols].reshape(rows * cols, channels)
            running = running + jnp.dot(window_piece, w_space[row_step, col_step], preferred_element_type=jnp.float32)
    return running.reshape(rows, cols, channels).astype(jnp.bfloat16)

def attend(block, w_qkv, w_out):
    frames, pixels, channels = block.shape
    head_size = channels // HEADS
    flattened = block.reshape(frames * pixels, channels)
    projected = jnp.dot(flattened, w_qkv, preferred_element_type=jnp.float32).astype(jnp.bfloat16)
    projected = projected.reshape(frames, pixels, 3, HEADS, head_size)
    query_rows = projected[:, :, 0].astype(jnp.float32)
    key_rows = projected[:, :, 1].astype(jnp.float32)
    value_rows = projected[:, :, 2].astype(jnp.float32)
    scores = jnp.einsum('fphd,gphd->phfg', query_rows, key_rows) / math.sqrt(head_size)
    weights = jax.nn.softmax(scores, axis=-1).astype(jnp.bfloat16)
    context = jnp.einsum('phfg,gphd->fphd', weights.astype(jnp.float32), value_rows).astype(jnp.bfloat16)
    context = context.reshape(frames * pixels, channels)
    result = flattened.astype(jnp.float32) + jnp.dot(context, w_out, preferred_element_type=jnp.float32)
    return result.reshape(frames, pixels, channels).astype(jnp.bfloat16)

def reference(video, w_space, w_time, norm_gain, norm_bias, w_qkv, w_out):
    spatial = lax.map(lambda frame: space_frame(frame, w_space), video)
    padded = jnp.pad(spatial, ((1, 1), (0, 0), (0, 0), (0, 0)))

    def time_frame(frame_index):
        window_piece = lax.dynamic_slice_in_dim(padded, frame_index, 3, 0)
        running = window_piece[1].astype(jnp.float32).reshape(HEIGHT * WIDTH, C)
        for tap in range(3):
            running = running + jnp.dot(window_piece[tap].reshape(HEIGHT * WIDTH, C), w_time[tap], preferred_element_type=jnp.float32)
        return running.reshape(HEIGHT, WIDTH, C).astype(jnp.bfloat16)
    temporal = lax.map(time_frame, jnp.arange(FRAMES).astype(jnp.int32))
    grouped = temporal.astype(jnp.float32).reshape(FRAMES * HEIGHT * WIDTH, GROUPS, C // GROUPS)
    cell_count = float(FRAMES * HEIGHT * WIDTH * (C // GROUPS))
    group_mean = lax.optimization_barrier(jnp.sum(grouped, axis=(0, 2))) / cell_count
    centered = grouped - group_mean[None, :, None]
    group_var = lax.optimization_barrier(jnp.sum(centered * centered, axis=(0, 2))) / cell_count
    scaled = centered * lax.rsqrt(group_var + 1e-05)[None, :, None]
    scaled = scaled.reshape(FRAMES * HEIGHT * WIDTH, C) * norm_gain + norm_bias
    normed = jax.nn.silu(scaled).astype(jnp.bfloat16).reshape(FRAMES, HEIGHT * WIDTH, C)
    block_rows = math.gcd(HEIGHT * WIDTH, 512)
    blocks = HEIGHT * WIDTH // block_rows
    stacked = normed.reshape(FRAMES, blocks, block_rows, C).transpose(1, 0, 2, 3)
    outcome = lax.map(lambda block: attend(block, w_qkv, w_out), stacked)
    return outcome.transpose(1, 0, 2, 3).reshape(FRAMES, HEIGHT, WIDTH, C)
```

```python
import functools
import math

import jax
import jax.numpy as jnp
from jax import lax
from jax.experimental import pallas as pl
from jax.experimental.pallas import tpu as pltpu
from jax.sharding import PartitionSpec as P

HEADS = 8
GROUPS = 32
EPS = 1e-5
MESH = pl.DeviceIdType.MESH
STEPS = [(dr, dc) for dr in (-1, 0, 1) for dc in (-1, 0, 1) if (dr, dc) != (0, 0)]


def dot(a, b):
    return jnp.dot(a, b, preferred_element_type=jnp.float32)


def inside(index, size):
    return jnp.logical_and(index >= 0, index < size)


def kernel(
    sizes, x_ref, wsp_ref, wt_ref, gain_ref, bias_ref, wqkv_ref, wout_ref, out_ref,
    pad, spat, edge_out, edge_in, tmp, piece, recv, stage, qkv, ctx, normed_buf,
    stat, ex_t, ex_h, ex_w,
    load_sem, halo_send, halo_recv, edge_send, edge_recv, fwd_send, fwd_recv,
    back_send, back_recv, t_send, t_recv, h_send, h_recv, w_send, w_recv,
):
    nt, nh, nw = sizes
    rows, cols, frames, channels = x_ref.shape
    span = rows // nt
    unit = cols * frames
    total = nt * frames
    head = channels // HEADS
    t, h, w = (lax.axis_index(name) for name in ("tm", "height", "width"))

    barrier = pltpu.get_barrier_semaphore()
    count = 0
    for dr, dc in STEPS:
        there = jnp.logical_and(inside(h + dr, nh), inside(w + dc, nw))

        @pl.when(there)
        def _(dr=dr, dc=dc):
            pl.semaphore_signal(barrier, inc=1, device_id=(t, h + dr, w + dc), device_id_type=MESH)

        count = count + there.astype(jnp.int32)
    for k in range(1, nt):
        pl.semaphore_signal(barrier, inc=1, device_id=(lax.rem(t + k, nt), h, w), device_id_type=MESH)
    for k in range(1, nh):
        pl.semaphore_signal(barrier, inc=1, device_id=(t, lax.rem(h + k, nh), w), device_id_type=MESH)
    for k in range(1, nw):
        pl.semaphore_signal(barrier, inc=1, device_id=(t, h, lax.rem(w + k, nw)), device_id_type=MESH)

    load = pltpu.make_async_copy(x_ref, pad.at[pl.ds(1, rows), pl.ds(1, cols)], load_sem)
    load.start()
    pl.semaphore_wait(barrier, count + (nt - 1) + (nh - 1) + (nw - 1))

    def span_of(step, size):
        src = {-1: pl.ds(0, 1), 0: pl.ds(0, size), 1: pl.ds(size - 1, 1)}[step]
        dst = {-1: pl.ds(size + 1, 1), 0: pl.ds(1, size), 1: pl.ds(0, 1)}[step]
        return src, dst

    def halo(index, sign):
        dr, dc = STEPS[index]
        (src_r, dst_r), (src_c, dst_c) = span_of(dr, rows), span_of(dc, cols)
        return pltpu.make_async_remote_copy(
            src_ref=x_ref.at[src_r, src_c], dst_ref=pad.at[dst_r, dst_c],
            send_sem=halo_send.at[index], recv_sem=halo_recv.at[index],
            device_id=(t, h + sign * dr, w + sign * dc), device_id_type=MESH,
        )

    for index, (dr, dc) in enumerate(STEPS):
        @pl.when(jnp.logical_and(inside(h + dr, nh), inside(w + dc, nw)))
        def _(index=index):
            halo(index, 1).start()
    for index, (dr, dc) in enumerate(STEPS):
        @pl.when(jnp.logical_not(jnp.logical_and(inside(h - dr, nh), inside(w - dc, nw))))
        def _(dr=dr, dc=dc):
            dst_r, dst_c = span_of(dr, rows)[1], span_of(dc, cols)[1]
            pad[dst_r, dst_c] = jnp.zeros((dst_r.size, dst_c.size, frames, channels), pad.dtype)
    load.wait()
    for index, (dr, dc) in enumerate(STEPS):
        @pl.when(jnp.logical_and(inside(h - dr, nh), inside(w - dc, nw)))
        def _(index=index):
            halo(index, -1).wait_recv()

    block = 2 if rows % 2 == 0 else 1

    def conv_step(step, carry):
        r = step * block
        acc = jnp.zeros((block * unit, channels), jnp.float32)
        for i in range(3):
            for j in range(3):
                taps = pad[pl.ds(r + i, block), pl.ds(j, cols)].reshape(block * unit, channels)
                acc = acc + dot(taps, wsp_ref[i, j])
        value = acc.astype(jnp.bfloat16)
        spat[pl.ds(r, block)] = value.reshape(block, unit, channels)
        lanes = tmp.shape[2]
        for c in range(channels // lanes):
            tmp[c] = value[:, c * lanes:(c + 1) * lanes].astype(jnp.float32)
        for b in range(block):
            for side, frame in ((0, 0), (1, frames - 1)):
                edge_out[side, r + b] = jnp.concatenate(
                    [tmp[c, pl.ds(b * unit + frame, cols, stride=frames), :]
                     for c in range(channels // lanes)], axis=1
                ).astype(jnp.bfloat16)
        return carry

    lax.fori_loop(0, rows // block, conv_step, 0)

    def edge(side, sign):
        step = (-1, 1)[side]
        return pltpu.make_async_remote_copy(
            src_ref=edge_out.at[side], dst_ref=edge_in.at[side],
            send_sem=edge_send.at[side], recv_sem=edge_recv.at[side],
            device_id=(t + sign * step, h, w), device_id_type=MESH,
        )

    for side, step in ((0, -1), (1, 1)):
        @pl.when(inside(t + step, nt))
        def _(side=side):
            edge(side, 1).start()

        @pl.when(jnp.logical_not(inside(t - step, nt)))
        def _(side=side):
            edge_in[side] = jnp.zeros(edge_in.shape[1:], edge_in.dtype)
    for side, step in ((0, -1), (1, 1)):
        @pl.when(inside(t - step, nt))
        def _(side=side):
            edge(side, -1).wait_recv()

    stat[...] = jnp.zeros_like(stat)
    frame_of = lax.rem(lax.broadcasted_iota(jnp.int32, (unit, channels), 0), frames)

    def forward(k, s):
        to = lax.rem(t + k, nt)
        return pltpu.make_async_remote_copy(
            src_ref=piece.at[k, s], dst_ref=recv.at[t, s],
            send_sem=fwd_send.at[k, s], recv_sem=fwd_recv.at[k, s],
            device_id=(to, h, w), device_id_type=MESH,
        )

    def time_step(s, carry):
        for k in list(range(1, nt)) + [0]:
            r = lax.rem(t + k, nt) * span + s
            here = spat[r]
            before = pltpu.roll(dot(here, wt_ref[0]), 1, 0)
            after = pltpu.roll(dot(here, wt_ref[2]), unit - 1, 0)
            spread = lambda v: jnp.broadcast_to(v[:, None, :], (cols, frames, channels)).reshape(unit, channels)
            first = spread(dot(edge_in[1, r], wt_ref[0]))
            last = spread(dot(edge_in[0, r], wt_ref[2]))
            value = here.astype(jnp.float32) + dot(here, wt_ref[1])
            value = value + jnp.where(frame_of == 0, first, before)
            value = value + jnp.where(frame_of == frames - 1, last, after)
            value = value.astype(jnp.bfloat16)
            if k:
                piece[k, s] = value
                forward(k, s).start()
            else:
                recv[t, s] = value
            wide = value.astype(jnp.float32)
            stat[0:1] += jnp.sum(wide, axis=0, keepdims=True)
            stat[1:2] += jnp.sum(wide * wide, axis=0, keepdims=True)
        return carry

    lax.fori_loop(0, span, time_step, 0)

    def exchange(slots, size, me, device, send, arrive):
        slots[me] = stat[...]

        def copy(k):
            return pltpu.make_async_remote_copy(
                src_ref=slots.at[me], dst_ref=slots.at[me],
                send_sem=send.at[k], recv_sem=arrive.at[k],
                device_id=device(lax.rem(me + k, size)), device_id_type=MESH,
            )

        def landed(k):
            other = lax.rem(me + size - k, size)
            return pltpu.make_async_remote_copy(
                src_ref=slots.at[other], dst_ref=slots.at[other],
                send_sem=send.at[k], recv_sem=arrive.at[k],
                device_id=device(other), device_id_type=MESH,
            )

        for k in range(1, size):
            copy(k).start()
        for k in range(1, size):
            landed(k).wait_recv()
        stat[...] = jnp.sum(slots[...], axis=0)
        for k in range(1, size):
            copy(k).wait_send()

    exchange(ex_t, nt, t, lambda o: (o, h, w), t_send, t_recv)
    exchange(ex_h, nh, h, lambda o: (t, o, w), h_send, h_recv)
    exchange(ex_w, nw, w, lambda o: (t, h, o), w_send, w_recv)

    cells = float(total * rows * nh * cols * nw * (channels // GROUPS))
    size = channels // GROUPS
    same = (
        lax.broadcasted_iota(jnp.int32, (channels, channels), 0) // size
        == lax.broadcasted_iota(jnp.int32, (channels, channels), 1) // size
    ).astype(jnp.float32)
    sums = jnp.dot(
        stat[...], same, precision=lax.Precision.HIGHEST, preferred_element_type=jnp.float32
    ) / cells
    mean = sums[0:1]
    var = jnp.maximum(sums[1:2] - mean * mean, 0.0)
    gain = lax.rsqrt(var + EPS) * gain_ref[...]
    bias = bias_ref[...]

    lane_head = lax.broadcasted_iota(jnp.int32, (total, channels), 1) // head
    factor = math.log2(math.e) / math.sqrt(head)

    def back(k, s):
        to = lax.rem(t + k, nt)
        return pltpu.make_async_remote_copy(
            src_ref=stage.at[to, s], dst_ref=out_ref.at[t, s],
            send_sem=back_send.at[k, s], recv_sem=back_recv.at[k, s],
            device_id=(to, h, w), device_id_type=MESH,
        )

    def attend_unit(s, carry):
        for k in range(1, nt):
            forward(k, s).wait_recv()
        for i in range(nt):
            v = (recv[i, s].astype(jnp.float32) - mean) * gain + bias
            v = (v / (1.0 + jnp.exp(-v))).astype(jnp.bfloat16)
            normed_buf[:, i * frames:(i + 1) * frames] = v.reshape(cols, frames, channels)
        rows_in = normed_buf[...].reshape(cols * total, channels)
        qkv[...] = dot(rows_in, wqkv_ref[...]).astype(jnp.bfloat16).reshape(cols, total, 3 * channels)

        def pixel(p, inner):
            q = qkv[p, :, 0:channels]
            key = qkv[p, :, channels:2 * channels]
            value = qkv[p, :, 2 * channels:]
            spread = jnp.concatenate(
                [jnp.where(lane_head == i, q, jnp.zeros_like(q)) for i in range(HEADS)], axis=0
            )
            scores = lax.dot_general(
                key, spread, (((1,), (1,)), ((), ())), preferred_element_type=jnp.float32
            )
            top = jnp.max(scores, axis=0, keepdims=True)
            parts = jnp.exp2((scores - top) * factor)
            weights = (parts / jnp.sum(parts, axis=0, keepdims=True)).astype(jnp.bfloat16)
            mixed = lax.dot_general(
                weights, value, (((0,), (0,)), ((), ())), preferred_element_type=jnp.float32
            )
            result = jnp.zeros((total, channels), jnp.float32)
            for i in range(HEADS):
                result = jnp.where(lane_head == i, mixed[i * total:(i + 1) * total], result)
            ctx[p] = result.astype(jnp.bfloat16)
            return inner

        lax.fori_loop(0, cols, pixel, 0)
        done = normed_buf[...].astype(jnp.float32).reshape(cols * total, channels)
        done = done + dot(ctx[...].reshape(cols * total, channels), wout_ref[...])
        done = done.astype(jnp.bfloat16).reshape(cols, total, channels)
        for i in range(nt):
            stage[i, s] = done[:, i * frames:(i + 1) * frames].reshape(unit, channels)
        for k in range(1, nt):
            back(k, s).start()
        out_ref[t, s] = stage[t, s]
        return carry

    lax.fori_loop(0, span, attend_unit, 0)

    def drain(s, carry):
        for k in range(1, nt):
            back(k, s).wait_recv()
            back(k, s).wait_send()
            forward(k, s).wait_send()
        return carry

    lax.fori_loop(0, span, drain, 0)
    for index, (dr, dc) in enumerate(STEPS):
        @pl.when(jnp.logical_and(inside(h + dr, nh), inside(w + dc, nw)))
        def _(index=index):
            halo(index, 1).wait_send()
    for side, step in ((0, -1), (1, 1)):
        @pl.when(inside(t + step, nt))
        def _(side=side):
            edge(side, 1).wait_send()


def per_device(sizes, video, w_space, w_time, norm_gain, norm_bias, w_qkv, w_out):
    frames, rows, cols, channels = video.shape
    nt, nh, nw = sizes
    span = rows // nt
    unit = cols * frames
    total = nt * frames
    x = jnp.transpose(video, (1, 2, 0, 3))
    vmem = pl.BlockSpec(memory_space=pltpu.VMEM)
    bf16, f32, dma = jnp.bfloat16, jnp.float32, pltpu.SemaphoreType.DMA
    block = 2 if rows % 2 == 0 else 1
    pixels = rows * cols * frames
    lanes = math.gcd(channels, 128)
    out = pl.pallas_call(
        functools.partial(kernel, sizes),
        out_shape=jax.ShapeDtypeStruct((nt, span, unit, channels), bf16),
        in_specs=[pl.BlockSpec(memory_space=pl.ANY)] + [vmem] * 6,
        out_specs=vmem,
        scratch_shapes=[
            pltpu.VMEM((rows + 2, cols + 2, frames, channels), bf16),
            pltpu.VMEM((rows, unit, channels), bf16),
            pltpu.VMEM((2, rows, cols, channels), bf16),
            pltpu.VMEM((2, rows, cols, channels), bf16),
            pltpu.VMEM((channels // lanes, block * unit, lanes), f32),
            pltpu.VMEM((nt, span, unit, channels), bf16),
            pltpu.VMEM((nt, span, unit, channels), bf16),
            pltpu.VMEM((nt, span, unit, channels), bf16),
            pltpu.VMEM((cols, total, 3 * channels), bf16),
            pltpu.VMEM((cols, total, channels), bf16),
            pltpu.VMEM((cols, total, channels), bf16),
            pltpu.VMEM((8, channels), f32),
            pltpu.VMEM((nt, 8, channels), f32),
            pltpu.VMEM((nh, 8, channels), f32),
            pltpu.VMEM((nw, 8, channels), f32),
            dma, dma((len(STEPS),)), dma((len(STEPS),)), dma((2,)), dma((2,)),
            dma((nt, span)), dma((nt, span)), dma((nt, span)), dma((nt, span)),
            dma((nt,)), dma((nt,)), dma((nh,)), dma((nh,)), dma((nw,)), dma((nw,)),
        ],
        compiler_params=pltpu.CompilerParams(
            collective_id=0, has_side_effects=True, vmem_limit_bytes=52 * 1024 * 1024
        ),
        cost_estimate=pl.CostEstimate(
            flops=2 * pixels * channels * channels * 20,
            bytes_accessed=4 * pixels * channels, transcendentals=pixels * 64 * HEADS,
        ),
    )(
        x, w_space, w_time, norm_gain.reshape(1, channels), norm_bias.reshape(1, channels), w_qkv, w_out
    )
    return jnp.transpose(out.reshape(rows, cols, frames, channels), (2, 0, 1, 3))


def solution(mesh):
    sizes = tuple(mesh.shape[name] for name in ("tm", "height", "width"))
    placed = (P("tm", "height", "width", None), P(), P(), P(), P(), P(), P())
    return jax.shard_map(
        functools.partial(per_device, sizes),
        mesh=mesh,
        in_specs=placed,
        out_specs=P("tm", "height", "width", None),
        check_vma=False,
    )
```

```python
import functools
import math

import jax
import jax.numpy as jnp
from jax import lax
from jax.experimental import pallas as pl
from jax.experimental.pallas import tpu as pltpu
from jax.sharding import PartitionSpec as P

HEADS = 8
GROUPS = 32
EPS = 1e-5
MESH = pl.DeviceIdType.MESH
STEPS = [(dr, dc) for dr in (-1, 0, 1) for dc in (-1, 0, 1) if (dr, dc) != (0, 0)]


def dot(a, b):
    return jnp.dot(a, b, preferred_element_type=jnp.float32)


def inside(index, size):
    return jnp.logical_and(index >= 0, index < size)


def kernel(
    sizes, x_ref, wsp_ref, wt_ref, gain_ref, bias_ref, wqkv_ref, wout_ref, out_ref,
    pad, spat, edge_out, edge_in, tmp, piece, recv, stage, qkv, ctx, normed_buf,
    stat, ex_t, ex_h, ex_w,
    load_sem, halo_send, halo_recv, edge_send, edge_recv, fwd_send, fwd_recv,
    back_send, back_recv, t_send, t_recv, h_send, h_recv, w_send, w_recv,
):
    nt, nh, nw = sizes
    rows, cols, frames, channels = x_ref.shape
    span = rows // nt
    unit = cols * frames
    total = nt * frames
    head = channels // HEADS
    t, h, w = (lax.axis_index(name) for name in ("tm", "height", "width"))

    barrier = pltpu.get_barrier_semaphore()
    count = 0
    for dr, dc in STEPS:
        there = jnp.logical_and(inside(h + dr, nh), inside(w + dc, nw))

        @pl.when(there)
        def _(dr=dr, dc=dc):
            pl.semaphore_signal(barrier, inc=1, device_id=(t, h + dr, w + dc), device_id_type=MESH)

        count = count + there.astype(jnp.int32)
    for k in range(1, nt):
        pl.semaphore_signal(barrier, inc=1, device_id=(lax.rem(t + k, nt), h, w), device_id_type=MESH)
    for k in range(1, nh):
        pl.semaphore_signal(barrier, inc=1, device_id=(t, lax.rem(h + k, nh), w), device_id_type=MESH)
    for k in range(1, nw):
        pl.semaphore_signal(barrier, inc=1, device_id=(t, h, lax.rem(w + k, nw)), device_id_type=MESH)

    load = pltpu.make_async_copy(x_ref, pad.at[pl.ds(1, rows), pl.ds(1, cols)], load_sem)
    load.start()
    pl.semaphore_wait(barrier, count + (nt - 1) + (nh - 1) + (nw - 1))

    def span_of(step, size):
        src = {-1: pl.ds(0, 1), 0: pl.ds(0, size), 1: pl.ds(size - 1, 1)}[step]
        dst = {-1: pl.ds(size + 1, 1), 0: pl.ds(1, size), 1: pl.ds(0, 1)}[step]
        return src, dst

    def halo(index, sign):
        dr, dc = STEPS[index]
        (src_r, dst_r), (src_c, dst_c) = span_of(dr, rows), span_of(dc, cols)
        return pltpu.make_async_remote_copy(
            src_ref=x_ref.at[src_r, src_c], dst_ref=pad.at[dst_r, dst_c],
            send_sem=halo_send.at[index], recv_sem=halo_recv.at[index],
            device_id=(t, h + sign * dr, w + sign * dc), device_id_type=MESH,
        )

    for index, (dr, dc) in enumerate(STEPS):
        @pl.when(jnp.logical_and(inside(h + dr, nh), inside(w + dc, nw)))
        def _(index=index):
            halo(index, 1).start()
    for index, (dr, dc) in enumerate(STEPS):
        @pl.when(jnp.logical_not(jnp.logical_and(inside(h - dr, nh), inside(w - dc, nw))))
        def _(dr=dr, dc=dc):
            dst_r, dst_c = span_of(dr, rows)[1], span_of(dc, cols)[1]
            pad[dst_r, dst_c] = jnp.zeros((dst_r.size, dst_c.size, frames, channels), pad.dtype)
    load.wait()
    for index, (dr, dc) in enumerate(STEPS):
        @pl.when(jnp.logical_and(inside(h - dr, nh), inside(w - dc, nw)))
        def _(index=index):
            halo(index, -1).wait_recv()

    block = 2 if rows % 2 == 0 else 1

    def conv_step(step, carry):
        r = step * block
        acc = jnp.zeros((block * unit, channels), jnp.float32)
        for i in range(3):
            for j in range(3):
                taps = pad[pl.ds(r + i, block), pl.ds(j, cols)].reshape(block * unit, channels)
                acc = acc + dot(taps, wsp_ref[i, j])
        value = acc.astype(jnp.bfloat16)
        spat[pl.ds(r, block)] = value.reshape(block, unit, channels)
        lanes = tmp.shape[2]
        for c in range(channels // lanes):
            tmp[c] = value[:, c * lanes:(c + 1) * lanes].astype(jnp.float32)
        for b in range(block):
            for side, frame in ((0, 0), (1, frames - 1)):
                edge_out[side, r + b] = jnp.concatenate(
                    [tmp[c, pl.ds(b * unit + frame, cols, stride=frames), :]
                     for c in range(channels // lanes)], axis=1
                ).astype(jnp.bfloat16)
        return carry

    lax.fori_loop(0, rows // block, conv_step, 0)

    def edge(side, sign):
        step = (-1, 1)[side]
        return pltpu.make_async_remote_copy(
            src_ref=edge_out.at[side], dst_ref=edge_in.at[side],
            send_sem=edge_send.at[side], recv_sem=edge_recv.at[side],
            device_id=(t + sign * step, h, w), device_id_type=MESH,
        )

    for side, step in ((0, -1), (1, 1)):
        @pl.when(inside(t + step, nt))
        def _(side=side):
            edge(side, 1).start()

        @pl.when(jnp.logical_not(inside(t - step, nt)))
        def _(side=side):
            edge_in[side] = jnp.zeros(edge_in.shape[1:], edge_in.dtype)
    for side, step in ((0, -1), (1, 1)):
        @pl.when(inside(t - step, nt))
        def _(side=side):
            edge(side, -1).wait_recv()

    stat[...] = jnp.zeros_like(stat)
    frame_of = lax.rem(lax.broadcasted_iota(jnp.int32, (unit, channels), 0), frames)

    def forward(k, s):
        to = lax.rem(t + k, nt)
        return pltpu.make_async_remote_copy(
            src_ref=piece.at[k, s], dst_ref=recv.at[t, s],
            send_sem=fwd_send.at[k, s], recv_sem=fwd_recv.at[k, s],
            device_id=(to, h, w), device_id_type=MESH,
        )

    def time_step(s, carry):
        for k in list(range(1, nt)) + [0]:
            r = lax.rem(t + k, nt) * span + s
            here = spat[r]
            before = pltpu.roll(dot(here, wt_ref[0]), 1, 0)
            after = pltpu.roll(dot(here, wt_ref[2]), unit - 1, 0)
            spread = lambda v: jnp.broadcast_to(v[:, None, :], (cols, frames, channels)).reshape(unit, channels)
            first = spread(dot(edge_in[1, r], wt_ref[0]))
            last = spread(dot(edge_in[0, r], wt_ref[2]))
            value = here.astype(jnp.float32) + dot(here, wt_ref[1])
            value = value + jnp.where(frame_of == 0, first, before)
            value = value + jnp.where(frame_of == frames - 1, last, after)
            value = value.astype(jnp.bfloat16)
            if k:
                piece[k, s] = value
                forward(k, s).start()
            else:
                recv[t, s] = value
            wide = value.astype(jnp.float32)
            stat[0:1] += jnp.sum(wide, axis=0, keepdims=True)
            stat[1:2] += jnp.sum(wide * wide, axis=0, keepdims=True)
        return carry

    lax.fori_loop(0, span, time_step, 0)

    def exchange(slots, size, me, device, send, arrive):
        slots[me] = stat[...]

        def copy(k):
            return pltpu.make_async_remote_copy(
                src_ref=slots.at[me], dst_ref=slots.at[me],
                send_sem=send.at[k], recv_sem=arrive.at[k],
                device_id=device(lax.rem(me + k, size)), device_id_type=MESH,
            )

        def landed(k):
            other = lax.rem(me + size - k, size)
            return pltpu.make_async_remote_copy(
                src_ref=slots.at[other], dst_ref=slots.at[other],
                send_sem=send.at[k], recv_sem=arrive.at[k],
                device_id=device(other), device_id_type=MESH,
            )

        for k in range(1, size):
            copy(k).start()
        for k in range(1, size):
            landed(k).wait_recv()
        stat[...] = jnp.sum(slots[...], axis=0)
        for k in range(1, size):
            copy(k).wait_send()

    exchange(ex_t, nt, t, lambda o: (o, h, w), t_send, t_recv)
    exchange(ex_h, nh, h, lambda o: (t, o, w), h_send, h_recv)
    exchange(ex_w, nw, w, lambda o: (t, h, o), w_send, w_recv)

    cells = float(total * rows * nh * cols * nw * (channels // GROUPS))
    size = channels // GROUPS
    same = (
        lax.broadcasted_iota(jnp.int32, (channels, channels), 0) // size
        == lax.broadcasted_iota(jnp.int32, (channels, channels), 1) // size
    ).astype(jnp.float32)
    sums = jnp.dot(
        stat[...], same, precision=lax.Precision.HIGHEST, preferred_element_type=jnp.float32
    ) / cells
    mean = sums[0:1]
    var = jnp.maximum(sums[1:2] - mean * mean, 0.0)
    gain = lax.rsqrt(var + EPS) * gain_ref[...]
    bias = bias_ref[...]

    lane_head = lax.broadcasted_iota(jnp.int32, (total, channels), 1) // head
    within = 2 if HEADS % 2 == 0 else 1
    pairs = HEADS // within
    together = math.gcd(cols, 4)

    def split_pairs(v):
        return jnp.concatenate(
            [jnp.where(lane_head // within == i, v, jnp.zeros_like(v)) for i in range(pairs)], axis=0
        )

    def split_within(v):
        return jnp.concatenate(
            [jnp.where(lane_head % within == i, v, jnp.zeros_like(v)) for i in range(within)], axis=0
        )

    factor = math.log2(math.e) / math.sqrt(head)

    def back(k, s):
        to = lax.rem(t + k, nt)
        return pltpu.make_async_remote_copy(
            src_ref=stage.at[to, s], dst_ref=out_ref.at[t, s],
            send_sem=back_send.at[k, s], recv_sem=back_recv.at[k, s],
            device_id=(to, h, w), device_id_type=MESH,
        )

    def attend_unit(s, carry):
        for k in range(1, nt):
            forward(k, s).wait_recv()
        for i in range(nt):
            v = (recv[i, s].astype(jnp.float32) - mean) * gain + bias
            v = (v / (1.0 + jnp.exp(-v))).astype(jnp.bfloat16)
            normed_buf[:, i * frames:(i + 1) * frames] = v.reshape(cols, frames, channels)
        rows_in = normed_buf[...].reshape(cols * total, channels)
        qkv[...] = dot(rows_in, wqkv_ref[...]).astype(jnp.bfloat16).reshape(cols, total, 3 * channels)

        def pixel_group(g, inner):
            ps = [g * together + i for i in range(together)]
            scores = []
            for p in ps:
                q = qkv[p, :, 0:channels]
                key = qkv[p, :, channels:2 * channels]
                scores.append(lax.dot_general(
                    split_pairs(key), split_within(q), (((1,), (1,)), ((), ())),
                    preferred_element_type=jnp.float32,
                ).reshape(pairs, total, within * total))
            weights = []
            for value in scores:
                top = jnp.max(value, axis=1, keepdims=True)
                parts = jnp.exp2((value - top) * factor)
                share = 1.0 / jnp.sum(parts, axis=1, keepdims=True)
                weights.append((parts * share).astype(jnp.bfloat16).reshape(pairs * total, within * total))
            for p, value in zip(ps, weights):
                mixed = lax.dot_general(
                    value, split_pairs(qkv[p, :, 2 * channels:]), (((0,), (0,)), ((), ())),
                    preferred_element_type=jnp.float32,
                )
                result = mixed[0:total]
                for i in range(1, within):
                    result = jnp.where(lane_head % within == i, mixed[i * total:(i + 1) * total], result)
                ctx[p] = result.astype(jnp.bfloat16)
            return inner

        lax.fori_loop(0, cols // together, pixel_group, 0)
        done = normed_buf[...].astype(jnp.float32).reshape(cols * total, channels)
        done = done + dot(ctx[...].reshape(cols * total, channels), wout_ref[...])
        done = done.astype(jnp.bfloat16).reshape(cols, total, channels)
        for i in range(nt):
            stage[i, s] = done[:, i * frames:(i + 1) * frames].reshape(unit, channels)
        for k in range(1, nt):
            back(k, s).start()
        out_ref[t, s] = stage[t, s]
        return carry

    lax.fori_loop(0, span, attend_unit, 0)

    def drain(s, carry):
        for k in range(1, nt):
            back(k, s).wait_recv()
            back(k, s).wait_send()
            forward(k, s).wait_send()
        return carry

    lax.fori_loop(0, span, drain, 0)
    for index, (dr, dc) in enumerate(STEPS):
        @pl.when(jnp.logical_and(inside(h + dr, nh), inside(w + dc, nw)))
        def _(index=index):
            halo(index, 1).wait_send()
    for side, step in ((0, -1), (1, 1)):
        @pl.when(inside(t + step, nt))
        def _(side=side):
            edge(side, 1).wait_send()


def per_device(sizes, video, w_space, w_time, norm_gain, norm_bias, w_qkv, w_out):
    frames, rows, cols, channels = video.shape
    nt, nh, nw = sizes
    span = rows // nt
    unit = cols * frames
    total = nt * frames
    x = jnp.transpose(video, (1, 2, 0, 3))
    vmem = pl.BlockSpec(memory_space=pltpu.VMEM)
    bf16, f32, dma = jnp.bfloat16, jnp.float32, pltpu.SemaphoreType.DMA
    block = 2 if rows % 2 == 0 else 1
    pixels = rows * cols * frames
    lanes = math.gcd(channels, 128)
    out = pl.pallas_call(
        functools.partial(kernel, sizes),
        out_shape=jax.ShapeDtypeStruct((nt, span, unit, channels), bf16),
        in_specs=[pl.BlockSpec(memory_space=pl.ANY)] + [vmem] * 6,
        out_specs=vmem,
        scratch_shapes=[
            pltpu.VMEM((rows + 2, cols + 2, frames, channels), bf16),
            pltpu.VMEM((rows, unit, channels), bf16),
            pltpu.VMEM((2, rows, cols, channels), bf16),
            pltpu.VMEM((2, rows, cols, channels), bf16),
            pltpu.VMEM((channels // lanes, block * unit, lanes), f32),
            pltpu.VMEM((nt, span, unit, channels), bf16),
            pltpu.VMEM((nt, span, unit, channels), bf16),
            pltpu.VMEM((nt, span, unit, channels), bf16),
            pltpu.VMEM((cols, total, 3 * channels), bf16),
            pltpu.VMEM((cols, total, channels), bf16),
            pltpu.VMEM((cols, total, channels), bf16),
            pltpu.VMEM((8, channels), f32),
            pltpu.VMEM((nt, 8, channels), f32),
            pltpu.VMEM((nh, 8, channels), f32),
            pltpu.VMEM((nw, 8, channels), f32),
            dma, dma((len(STEPS),)), dma((len(STEPS),)), dma((2,)), dma((2,)),
            dma((nt, span)), dma((nt, span)), dma((nt, span)), dma((nt, span)),
            dma((nt,)), dma((nt,)), dma((nh,)), dma((nh,)), dma((nw,)), dma((nw,)),
        ],
        compiler_params=pltpu.CompilerParams(
            collective_id=0, has_side_effects=True, vmem_limit_bytes=52 * 1024 * 1024
        ),
        cost_estimate=pl.CostEstimate(
            flops=2 * pixels * channels * channels * 20,
            bytes_accessed=4 * pixels * channels, transcendentals=pixels * 64 * HEADS,
        ),
    )(
        x, w_space, w_time, norm_gain.reshape(1, channels), norm_bias.reshape(1, channels), w_qkv, w_out
    )
    return jnp.transpose(out.reshape(rows, cols, frames, channels), (2, 0, 1, 3))


def solution(mesh):
    sizes = tuple(mesh.shape[name] for name in ("tm", "height", "width"))
    placed = (P("tm", "height", "width", None), P(), P(), P(), P(), P(), P())
    return jax.shard_map(
        functools.partial(per_device, sizes),
        mesh=mesh,
        in_specs=placed,
        out_specs=P("tm", "height", "width", None),
        check_vma=False,
    )
```

```python
import functools
import math

import jax
import jax.numpy as jnp
from jax import lax
from jax.experimental import pallas as pl
from jax.experimental.pallas import tpu as pltpu
from jax.sharding import PartitionSpec as P

HEADS = 8
GROUPS = 32
EPS = 1e-5
MESH = pl.DeviceIdType.MESH
STEPS = [(dr, dc) for dr in (-1, 0, 1) for dc in (-1, 0, 1) if (dr, dc) != (0, 0)]


def dot(a, b):
    return jnp.dot(a, b, preferred_element_type=jnp.float32)


def inside(index, size):
    return jnp.logical_and(index >= 0, index < size)


def kernel(
    sizes, x_ref, wsp_ref, wt_ref, gain_ref, bias_ref, wqkv_ref, wout_ref, out_ref,
    pad, spat, edge_out, edge_in, tmp, turn, turn_out, piece, recv, stage, qkv, ctx, normed_buf,
    stat, ex_t, ex_h, ex_w,
    halo_send, halo_recv, edge_send, edge_recv, fwd_send, fwd_recv,
    back_send, back_recv, t_send, t_recv, h_send, h_recv, w_send, w_recv,
):
    nt, nh, nw = sizes
    frames, rows, cols, channels = x_ref.shape
    span = rows // nt
    unit = cols * frames
    total = nt * frames
    head = channels // HEADS
    t, h, w = (lax.axis_index(name) for name in ("tm", "height", "width"))

    barrier = pltpu.get_barrier_semaphore()
    count = 0
    for dr, dc in STEPS:
        there = jnp.logical_and(inside(h + dr, nh), inside(w + dc, nw))

        @pl.when(there)
        def _(dr=dr, dc=dc):
            pl.semaphore_signal(barrier, inc=1, device_id=(t, h + dr, w + dc), device_id_type=MESH)

        count = count + there.astype(jnp.int32)
    for k in range(1, nt):
        pl.semaphore_signal(barrier, inc=1, device_id=(lax.rem(t + k, nt), h, w), device_id_type=MESH)
    for k in range(1, nh):
        pl.semaphore_signal(barrier, inc=1, device_id=(t, lax.rem(h + k, nh), w), device_id_type=MESH)
    for k in range(1, nw):
        pl.semaphore_signal(barrier, inc=1, device_id=(t, h, lax.rem(w + k, nw)), device_id_type=MESH)

    lanes = tmp.shape[2]
    halves = channels // lanes
    two = 2 if rows % 2 == 0 else 1

    def turn_in(step, carry):
        for b in range(two):
            r = step * two + b
            for c in range(halves):
                turn[b * halves + c] = x_ref[:, r, :, c * lanes:(c + 1) * lanes].astype(
                    jnp.float32
                ).reshape(unit, lanes)
            for i in range(cols):
                pad[r + 1, i + 1] = jnp.concatenate(
                    [turn[b * halves + c, pl.ds(i, frames, stride=cols), :] for c in range(halves)], axis=1
                ).astype(jnp.bfloat16)
        return carry

    lax.fori_loop(0, rows // two, turn_in, 0)
    pl.semaphore_wait(barrier, count + (nt - 1) + (nh - 1) + (nw - 1))

    def span_of(step, size):
        src = {-1: pl.ds(1, 1), 0: pl.ds(1, size), 1: pl.ds(size, 1)}[step]
        dst = {-1: pl.ds(size + 1, 1), 0: pl.ds(1, size), 1: pl.ds(0, 1)}[step]
        return src, dst

    def halo(index, sign):
        dr, dc = STEPS[index]
        (src_r, dst_r), (src_c, dst_c) = span_of(dr, rows), span_of(dc, cols)
        return pltpu.make_async_remote_copy(
            src_ref=pad.at[src_r, src_c], dst_ref=pad.at[dst_r, dst_c],
            send_sem=halo_send.at[index], recv_sem=halo_recv.at[index],
            device_id=(t, h + sign * dr, w + sign * dc), device_id_type=MESH,
        )

    for index, (dr, dc) in enumerate(STEPS):
        @pl.when(jnp.logical_and(inside(h + dr, nh), inside(w + dc, nw)))
        def _(index=index):
            halo(index, 1).start()
    for index, (dr, dc) in enumerate(STEPS):
        @pl.when(jnp.logical_not(jnp.logical_and(inside(h - dr, nh), inside(w - dc, nw))))
        def _(dr=dr, dc=dc):
            dst_r, dst_c = span_of(dr, rows)[1], span_of(dc, cols)[1]
            pad[dst_r, dst_c] = jnp.zeros((dst_r.size, dst_c.size, frames, channels), pad.dtype)
    for index, (dr, dc) in enumerate(STEPS):
        @pl.when(jnp.logical_and(inside(h - dr, nh), inside(w - dc, nw)))
        def _(index=index):
            halo(index, -1).wait_recv()

    block = 2 if nt % 2 == 0 else 1

    def edge(side, s, sign):
        step = (-1, 1)[side]
        return pltpu.make_async_remote_copy(
            src_ref=edge_out.at[side, s], dst_ref=edge_in.at[side, s],
            send_sem=edge_send.at[side, s], recv_sem=edge_recv.at[side, s],
            device_id=(t + sign * step, h, w), device_id_type=MESH,
        )

    def conv_round(s):
        for first in range(0, nt, block):
            acc = jnp.zeros((block * unit, channels), jnp.float32)
            for i in range(3):
                for j in range(3):
                    taps = jnp.concatenate(
                        [pad[(first + b) * span + s + i, pl.ds(j, cols)].reshape(unit, channels)
                         for b in range(block)], axis=0
                    )
                    acc = acc + dot(taps, wsp_ref[i, j])
            value = acc.astype(jnp.bfloat16)
            for b in range(block):
                k = first + b
                here = value[b * unit:(b + 1) * unit]
                spat[k * span + s] = here
                for c in range(halves):
                    tmp[k * halves + c] = here[:, c * lanes:(c + 1) * lanes].astype(jnp.float32)
                for side, frame in ((0, 0), (1, frames - 1)):
                    edge_out[side, s, k] = jnp.concatenate(
                        [tmp[k * halves + c, pl.ds(frame, cols, stride=frames), :] for c in range(halves)],
                        axis=1,
                    ).astype(jnp.bfloat16)
        for side, step in ((0, -1), (1, 1)):
            @pl.when(inside(t + step, nt))
            def _(side=side):
                edge(side, s, 1).start()

    for side, step in ((0, -1), (1, 1)):
        @pl.when(jnp.logical_not(inside(t - step, nt)))
        def _(side=side):
            edge_in[side] = jnp.zeros(edge_in.shape[1:], edge_in.dtype)

    stat[...] = jnp.zeros_like(stat)
    frame_of = lax.rem(lax.broadcasted_iota(jnp.int32, (unit, channels), 0), frames)

    def forward(k, s):
        to = lax.rem(t + k, nt)
        return pltpu.make_async_remote_copy(
            src_ref=piece.at[k, s], dst_ref=recv.at[t, s],
            send_sem=fwd_send.at[k, s], recv_sem=fwd_recv.at[k, s],
            device_id=(to, h, w), device_id_type=MESH,
        )

    def spread(v):
        return jnp.broadcast_to(v[:, None, :], (cols, frames, channels)).reshape(unit, channels)

    def time_round(s):
        for side, step in ((0, -1), (1, 1)):
            @pl.when(inside(t - step, nt))
            def _(side=side):
                edge(side, s, -1).wait_recv()
        for k in list(range(1, nt)) + [0]:
            chunk = lax.rem(t + k, nt)
            here = spat[chunk * span + s]
            before = pltpu.roll(dot(here, wt_ref[0]), 1, 0)
            after = pltpu.roll(dot(here, wt_ref[2]), unit - 1, 0)
            first = spread(dot(edge_in[1, s, chunk], wt_ref[0]))
            last = spread(dot(edge_in[0, s, chunk], wt_ref[2]))
            value = here.astype(jnp.float32) + dot(here, wt_ref[1])
            value = value + jnp.where(frame_of == 0, first, before)
            value = value + jnp.where(frame_of == frames - 1, last, after)
            value = value.astype(jnp.bfloat16)
            if k:
                piece[k, s] = value
                forward(k, s).start()
            else:
                recv[t, s] = value
            wide = value.astype(jnp.float32)
            stat[0:1] += jnp.sum(wide, axis=0, keepdims=True)
            stat[1:2] += jnp.sum(wide * wide, axis=0, keepdims=True)

    def both(s, carry):
        conv_round(s)
        time_round(s - 1)
        return carry

    conv_round(0)
    lax.fori_loop(1, span, both, 0)
    time_round(span - 1)

    def exchange(slots, size, me, device, send, arrive):
        slots[me] = stat[...]

        def copy(k):
            return pltpu.make_async_remote_copy(
                src_ref=slots.at[me], dst_ref=slots.at[me],
                send_sem=send.at[k], recv_sem=arrive.at[k],
                device_id=device(lax.rem(me + k, size)), device_id_type=MESH,
            )

        def landed(k):
            other = lax.rem(me + size - k, size)
            return pltpu.make_async_remote_copy(
                src_ref=slots.at[other], dst_ref=slots.at[other],
                send_sem=send.at[k], recv_sem=arrive.at[k],
                device_id=device(other), device_id_type=MESH,
            )

        for k in range(1, size):
            copy(k).start()
        for k in range(1, size):
            landed(k).wait_recv()
        stat[...] = jnp.sum(slots[...], axis=0)
        for k in range(1, size):
            copy(k).wait_send()

    exchange(ex_t, nt, t, lambda o: (o, h, w), t_send, t_recv)
    exchange(ex_h, nh, h, lambda o: (t, o, w), h_send, h_recv)
    exchange(ex_w, nw, w, lambda o: (t, h, o), w_send, w_recv)

    cells = float(total * rows * nh * cols * nw * (channels // GROUPS))
    size = channels // GROUPS
    same = (
        lax.broadcasted_iota(jnp.int32, (channels, channels), 0) // size
        == lax.broadcasted_iota(jnp.int32, (channels, channels), 1) // size
    ).astype(jnp.float32)
    sums = jnp.dot(
        stat[...], same, precision=lax.Precision.HIGHEST, preferred_element_type=jnp.float32
    ) / cells
    mean = sums[0:1]
    var = jnp.maximum(sums[1:2] - mean * mean, 0.0)
    gain = lax.rsqrt(var + EPS) * gain_ref[...]
    bias = bias_ref[...]

    lane_head = lax.broadcasted_iota(jnp.int32, (total, channels), 1) // head
    within = 2 if HEADS % 2 == 0 else 1
    pairs = HEADS // within
    together = math.gcd(cols, 4)

    def split_pairs(v):
        return jnp.concatenate(
            [jnp.where(lane_head // within == i, v, jnp.zeros_like(v)) for i in range(pairs)], axis=0
        )

    def split_within(v):
        return jnp.concatenate(
            [jnp.where(lane_head % within == i, v, jnp.zeros_like(v)) for i in range(within)], axis=0
        )

    factor = math.log2(math.e) / math.sqrt(head)

    def back(k, s):
        to = lax.rem(t + k, nt)
        return pltpu.make_async_remote_copy(
            src_ref=stage.at[to, s], dst_ref=out_ref.at[:, t * span + s],
            send_sem=back_send.at[k, s], recv_sem=back_recv.at[k, s],
            device_id=(to, h, w), device_id_type=MESH,
        )

    def attend_unit(s, carry):
        for k in range(1, nt):
            forward(k, s).wait_recv()
        for i in range(nt):
            v = (recv[i, s].astype(jnp.float32) - mean) * gain + bias
            v = (v / (1.0 + jnp.exp(-v))).astype(jnp.bfloat16)
            normed_buf[:, i * frames:(i + 1) * frames] = v.reshape(cols, frames, channels)
        rows_in = normed_buf[...].reshape(cols * total, channels)
        qkv[...] = dot(rows_in, wqkv_ref[...]).astype(jnp.bfloat16).reshape(cols, total, 3 * channels)

        def pixel_group(g, inner):
            ps = [g * together + i for i in range(together)]
            scores = []
            for p in ps:
                q = qkv[p, :, 0:channels]
                key = qkv[p, :, channels:2 * channels]
                scores.append(lax.dot_general(
                    split_pairs(key), split_within(q), (((1,), (1,)), ((), ())),
                    preferred_element_type=jnp.float32,
                ).reshape(pairs, total, within * total))
            weights = []
            for value in scores:
                top = jnp.max(value, axis=1, keepdims=True)
                parts = jnp.exp2((value - top) * factor)
                share = 1.0 / jnp.sum(parts, axis=1, keepdims=True)
                weights.append((parts * share).astype(jnp.bfloat16).reshape(pairs * total, within * total))
            for p, value in zip(ps, weights):
                mixed = lax.dot_general(
                    value, split_pairs(qkv[p, :, 2 * channels:]), (((0,), (0,)), ((), ())),
                    preferred_element_type=jnp.float32,
                )
                result = mixed[0:total]
                for i in range(1, within):
                    result = jnp.where(lane_head % within == i, mixed[i * total:(i + 1) * total], result)
                ctx[p] = result.astype(jnp.bfloat16)
            return inner

        lax.fori_loop(0, cols // together, pixel_group, 0)
        done = normed_buf[...].astype(jnp.float32).reshape(cols * total, channels)
        done = done + dot(ctx[...].reshape(cols * total, channels), wout_ref[...])
        for c in range(halves):
            turn_out[c] = done[:, c * lanes:(c + 1) * lanes]
        for i in range(nt):
            for f in range(frames):
                stage[i, s, f] = jnp.concatenate(
                    [turn_out[c, pl.ds(i * frames + f, cols, stride=total), :] for c in range(halves)],
                    axis=1,
                ).astype(jnp.bfloat16)
        for k in range(1, nt):
            back(k, s).start()
        out_ref[:, t * span + s] = stage[t, s]
        return carry

    lax.fori_loop(0, span, attend_unit, 0)

    def drain(s, carry):
        for k in range(1, nt):
            back(k, s).wait_recv()
            back(k, s).wait_send()
            forward(k, s).wait_send()
        return carry

    lax.fori_loop(0, span, drain, 0)
    for index, (dr, dc) in enumerate(STEPS):
        @pl.when(jnp.logical_and(inside(h + dr, nh), inside(w + dc, nw)))
        def _(index=index):
            halo(index, 1).wait_send()
    for side, step in ((0, -1), (1, 1)):
        @pl.when(inside(t + step, nt))
        def _(side=side):
            for s in range(span):
                edge(side, s, 1).wait_send()


def per_device(sizes, video, w_space, w_time, norm_gain, norm_bias, w_qkv, w_out):
    frames, rows, cols, channels = video.shape
    nt, nh, nw = sizes
    span = rows // nt
    unit = cols * frames
    total = nt * frames
    vmem = pl.BlockSpec(memory_space=pltpu.VMEM)
    bf16, f32, dma = jnp.bfloat16, jnp.float32, pltpu.SemaphoreType.DMA
    two = 2 if rows % 2 == 0 else 1
    pixels = rows * cols * frames
    lanes = math.gcd(channels, 128)
    halves = channels // lanes
    out = pl.pallas_call(
        functools.partial(kernel, sizes),
        out_shape=jax.ShapeDtypeStruct(video.shape, bf16),
        in_specs=[vmem] * 7,
        out_specs=vmem,
        scratch_shapes=[
            pltpu.VMEM((rows + 2, cols + 2, frames, channels), bf16),
            pltpu.VMEM((rows, unit, channels), bf16),
            pltpu.VMEM((2, span, nt, cols, channels), bf16),
            pltpu.VMEM((2, span, nt, cols, channels), bf16),
            pltpu.VMEM((nt * halves, unit, lanes), f32),
            pltpu.VMEM((two * halves, unit, lanes), f32),
            pltpu.VMEM((halves, cols * total, lanes), f32),
            pltpu.VMEM((nt, span, unit, channels), bf16),
            pltpu.VMEM((nt, span, unit, channels), bf16),
            pltpu.VMEM((nt, span, frames, cols, channels), bf16),
            pltpu.VMEM((cols, total, 3 * channels), bf16),
            pltpu.VMEM((cols, total, channels), bf16),
            pltpu.VMEM((cols, total, channels), bf16),
            pltpu.VMEM((8, channels), f32),
            pltpu.VMEM((nt, 8, channels), f32),
            pltpu.VMEM((nh, 8, channels), f32),
            pltpu.VMEM((nw, 8, channels), f32),
            dma((len(STEPS),)), dma((len(STEPS),)), dma((2, span)), dma((2, span)),
            dma((nt, span)), dma((nt, span)), dma((nt, span)), dma((nt, span)),
            dma((nt,)), dma((nt,)), dma((nh,)), dma((nh,)), dma((nw,)), dma((nw,)),
        ],
        compiler_params=pltpu.CompilerParams(
            collective_id=0, has_side_effects=True, vmem_limit_bytes=52 * 1024 * 1024
        ),
        cost_estimate=pl.CostEstimate(
            flops=2 * pixels * channels * channels * 20,
            bytes_accessed=4 * pixels * channels, transcendentals=pixels * 64 * HEADS,
        ),
    )(
        video, w_space, w_time, norm_gain.reshape(1, channels), norm_bias.reshape(1, channels), w_qkv, w_out
    )
    return out


def solution(mesh):
    sizes = tuple(mesh.shape[name] for name in ("tm", "height", "width"))
    placed = (P("tm", "height", "width", None), P(), P(), P(), P(), P(), P())
    return jax.shard_map(
        functools.partial(per_device, sizes),
        mesh=mesh,
        in_specs=placed,
        out_specs=P("tm", "height", "width", None),
        check_vma=False,
    )
```

```python
import functools
import math

import jax
import jax.numpy as jnp
from jax import lax
from jax.experimental import pallas as pl
from jax.experimental.pallas import tpu as pltpu
from jax.sharding import PartitionSpec as P

HEADS = 8
GROUPS = 32
EPS = 1e-5
MESH = pl.DeviceIdType.MESH
STEPS = [(dr, dc) for dr in (-1, 0, 1) for dc in (-1, 0, 1) if (dr, dc) != (0, 0)]


def dot(a, b):
    return jnp.dot(a, b, preferred_element_type=jnp.float32)


def inside(index, size):
    return jnp.logical_and(index >= 0, index < size)


def kernel(
    sizes, x_hbm, wsp_hbm, wt_hbm, gain_ref, bias_ref, wqkv_hbm, wout_hbm, out_ref,
    x_ref, wsp_ref, wt_ref, wqkv_ref, wout_ref,
    pad, spat, edge_out, edge_in, tmp, turn, turn_out, piece, recv, stage, qkv, ctx, normed_buf,
    stat, ex_t, ex_h, ex_w,
    load_sem, own_sem, halo_send, halo_recv, edge_send, edge_recv, fwd_send, fwd_recv,
    back_send, back_recv, t_send, t_recv, h_send, h_recv, w_send, w_recv,
):
    nt, nh, nw = sizes
    frames, rows, cols, channels = x_ref.shape
    span = rows // nt
    unit = cols * frames
    total = nt * frames
    head = channels // HEADS
    t, h, w = (lax.axis_index(name) for name in ("tm", "height", "width"))

    barrier = pltpu.get_barrier_semaphore()
    count = 0
    for dr, dc in STEPS:
        there = jnp.logical_and(inside(h + dr, nh), inside(w + dc, nw))

        @pl.when(there)
        def _(dr=dr, dc=dc):
            pl.semaphore_signal(barrier, inc=1, device_id=(t, h + dr, w + dc), device_id_type=MESH)

        count = count + there.astype(jnp.int32)
    for k in range(1, nt):
        pl.semaphore_signal(barrier, inc=1, device_id=(lax.rem(t + k, nt), h, w), device_id_type=MESH)
    for k in range(1, nh):
        pl.semaphore_signal(barrier, inc=1, device_id=(t, lax.rem(h + k, nh), w), device_id_type=MESH)
    for k in range(1, nw):
        pl.semaphore_signal(barrier, inc=1, device_id=(t, h, lax.rem(w + k, nw)), device_id_type=MESH)

    loads = [
        pltpu.make_async_copy(src, dst, load_sem.at[i])
        for i, (src, dst) in enumerate((
            (x_hbm, x_ref), (wsp_hbm, wsp_ref), (wt_hbm, wt_ref), (wqkv_hbm, wqkv_ref), (wout_hbm, wout_ref),
        ))
    ]
    for load in loads:
        load.start()
    loads[0].wait()

    lanes = tmp.shape[2]
    halves = channels // lanes
    two = 2 if rows % 2 == 0 else 1

    def turn_in(step, carry):
        for b in range(two):
            r = step * two + b
            for c in range(halves):
                turn[b * halves + c] = x_ref[:, r, :, c * lanes:(c + 1) * lanes].astype(
                    jnp.float32
                ).reshape(unit, lanes)
            for i in range(cols):
                pad[r + 1, i + 1] = jnp.concatenate(
                    [turn[b * halves + c, pl.ds(i, frames, stride=cols), :] for c in range(halves)], axis=1
                ).astype(jnp.bfloat16)
        return carry

    lax.fori_loop(0, rows // two, turn_in, 0)
    pl.semaphore_wait(barrier, count + (nt - 1) + (nh - 1) + (nw - 1))

    def span_of(step, size):
        src = {-1: pl.ds(1, 1), 0: pl.ds(1, size), 1: pl.ds(size, 1)}[step]
        dst = {-1: pl.ds(size + 1, 1), 0: pl.ds(1, size), 1: pl.ds(0, 1)}[step]
        return src, dst

    def halo(index, sign):
        dr, dc = STEPS[index]
        (src_r, dst_r), (src_c, dst_c) = span_of(dr, rows), span_of(dc, cols)
        return pltpu.make_async_remote_copy(
            src_ref=pad.at[src_r, src_c], dst_ref=pad.at[dst_r, dst_c],
            send_sem=halo_send.at[index], recv_sem=halo_recv.at[index],
            device_id=(t, h + sign * dr, w + sign * dc), device_id_type=MESH,
        )

    for index, (dr, dc) in enumerate(STEPS):
        @pl.when(jnp.logical_and(inside(h + dr, nh), inside(w + dc, nw)))
        def _(index=index):
            halo(index, 1).start()
    for index, (dr, dc) in enumerate(STEPS):
        @pl.when(jnp.logical_not(jnp.logical_and(inside(h - dr, nh), inside(w - dc, nw))))
        def _(dr=dr, dc=dc):
            dst_r, dst_c = span_of(dr, rows)[1], span_of(dc, cols)[1]
            pad[dst_r, dst_c] = jnp.zeros((dst_r.size, dst_c.size, frames, channels), pad.dtype)
    for index, (dr, dc) in enumerate(STEPS):
        @pl.when(jnp.logical_and(inside(h - dr, nh), inside(w - dc, nw)))
        def _(index=index):
            halo(index, -1).wait_recv()

    block = 2 if nt % 2 == 0 else 1

    def edge(side, s, sign):
        step = (-1, 1)[side]
        return pltpu.make_async_remote_copy(
            src_ref=edge_out.at[side, s], dst_ref=edge_in.at[side, s],
            send_sem=edge_send.at[side, s], recv_sem=edge_recv.at[side, s],
            device_id=(t + sign * step, h, w), device_id_type=MESH,
        )

    def conv_round(s):
        for first in range(0, nt, block):
            acc = jnp.zeros((block * unit, channels), jnp.float32)
            for i in range(3):
                for j in range(3):
                    taps = jnp.concatenate(
                        [pad[(first + b) * span + s + i, pl.ds(j, cols)].reshape(unit, channels)
                         for b in range(block)], axis=0
                    )
                    acc = acc + dot(taps, wsp_ref[i, j])
            value = acc.astype(jnp.bfloat16)
            for b in range(block):
                k = first + b
                here = value[b * unit:(b + 1) * unit]
                spat[k * span + s] = here
                for c in range(halves):
                    tmp[k * halves + c] = here[:, c * lanes:(c + 1) * lanes].astype(jnp.float32)
                for side, frame in ((0, 0), (1, frames - 1)):
                    edge_out[side, s, k] = jnp.concatenate(
                        [tmp[k * halves + c, pl.ds(frame, cols, stride=frames), :] for c in range(halves)],
                        axis=1,
                    ).astype(jnp.bfloat16)
        for side, step in ((0, -1), (1, 1)):
            @pl.when(inside(t + step, nt))
            def _(side=side):
                edge(side, s, 1).start()

    for side, step in ((0, -1), (1, 1)):
        @pl.when(jnp.logical_not(inside(t - step, nt)))
        def _(side=side):
            edge_in[side] = jnp.zeros(edge_in.shape[1:], edge_in.dtype)

    stat[...] = jnp.zeros_like(stat)
    frame_of = lax.rem(lax.broadcasted_iota(jnp.int32, (block * unit, channels), 0), frames)

    def forward(k, s):
        to = lax.rem(t + k, nt)
        return pltpu.make_async_remote_copy(
            src_ref=piece.at[k, s], dst_ref=recv.at[t, s],
            send_sem=fwd_send.at[k, s], recv_sem=fwd_recv.at[k, s],
            device_id=(to, h, w), device_id_type=MESH,
        )

    def spread(v):
        return jnp.broadcast_to(v[:, None, :], (block * cols, frames, channels)).reshape(block * unit, channels)

    def time_round(s):
        for side, step in ((0, -1), (1, 1)):
            @pl.when(inside(t - step, nt))
            def _(side=side):
                edge(side, s, -1).wait_recv()
        order = list(range(1, nt)) + [0]
        for place in range(0, nt, block):
            ks = order[place:place + block]
            chunks = [lax.rem(t + k, nt) for k in ks]
            here = jnp.concatenate([spat[chunk * span + s] for chunk in chunks], axis=0)
            ends = [jnp.concatenate([edge_in[side, s, chunk] for chunk in chunks], axis=0) for side in (0, 1)]
            value = here.astype(jnp.float32) + dot(here, wt_ref[1])
            before = pltpu.roll(dot(here, wt_ref[0]), 1, 0)
            value = value + jnp.where(frame_of == 0, spread(dot(ends[1], wt_ref[0])), before)
            after = pltpu.roll(dot(here, wt_ref[2]), block * unit - 1, 0)
            value = value + jnp.where(frame_of == frames - 1, spread(dot(ends[0], wt_ref[2])), after)
            value = value.astype(jnp.bfloat16)
            for b, k in enumerate(ks):
                part = value[b * unit:(b + 1) * unit]
                if k:
                    piece[k, s] = part
                    forward(k, s).start()
                else:
                    recv[t, s] = part
            wide = value.astype(jnp.float32)
            stat[0:1] += jnp.sum(wide, axis=0, keepdims=True)
            stat[1:2] += jnp.sum(wide * wide, axis=0, keepdims=True)

    def both(s, carry):
        conv_round(s)
        time_round(s - 1)
        return carry

    for load in loads[1:]:
        load.wait()
    conv_round(0)
    lax.fori_loop(1, span, both, 0)
    time_round(span - 1)

    def exchange(slots, size, me, device, send, arrive):
        slots[me] = stat[...]

        def copy(k):
            return pltpu.make_async_remote_copy(
                src_ref=slots.at[me], dst_ref=slots.at[me],
                send_sem=send.at[k], recv_sem=arrive.at[k],
                device_id=device(lax.rem(me + k, size)), device_id_type=MESH,
            )

        def landed(k):
            other = lax.rem(me + size - k, size)
            return pltpu.make_async_remote_copy(
                src_ref=slots.at[other], dst_ref=slots.at[other],
                send_sem=send.at[k], recv_sem=arrive.at[k],
                device_id=device(other), device_id_type=MESH,
            )

        for k in range(1, size):
            copy(k).start()
        for k in range(1, size):
            landed(k).wait_recv()
        stat[...] = jnp.sum(slots[...], axis=0)
        for k in range(1, size):
            copy(k).wait_send()

    exchange(ex_t, nt, t, lambda o: (o, h, w), t_send, t_recv)
    exchange(ex_h, nh, h, lambda o: (t, o, w), h_send, h_recv)
    exchange(ex_w, nw, w, lambda o: (t, h, o), w_send, w_recv)

    cells = float(total * rows * nh * cols * nw * (channels // GROUPS))
    size = channels // GROUPS
    same = (
        lax.broadcasted_iota(jnp.int32, (channels, channels), 0) // size
        == lax.broadcasted_iota(jnp.int32, (channels, channels), 1) // size
    ).astype(jnp.float32)
    sums = jnp.dot(
        stat[...], same, precision=lax.Precision.HIGHEST, preferred_element_type=jnp.float32
    ) / cells
    mean = sums[0:1]
    var = jnp.maximum(sums[1:2] - mean * mean, 0.0)
    gain = lax.rsqrt(var + EPS) * gain_ref[...]
    bias = bias_ref[...]

    lane_head = lax.broadcasted_iota(jnp.int32, (total, channels), 1) // head
    within = 2 if HEADS % 2 == 0 else 1
    pairs = HEADS // within
    together = math.gcd(cols, 8)

    def split_pairs(v):
        return jnp.concatenate(
            [jnp.where(lane_head // within == i, v, jnp.zeros_like(v)) for i in range(pairs)], axis=0
        )

    def split_within(v):
        return jnp.concatenate(
            [jnp.where(lane_head % within == i, v, jnp.zeros_like(v)) for i in range(within)], axis=0
        )

    factor = math.log2(math.e) / math.sqrt(head)

    def back(k, s):
        to = lax.rem(t + k, nt)
        return pltpu.make_async_remote_copy(
            src_ref=stage.at[to, s], dst_ref=out_ref.at[:, t * span + s],
            send_sem=back_send.at[k, s], recv_sem=back_recv.at[k, s],
            device_id=(to, h, w), device_id_type=MESH,
        )

    def own(s):
        return pltpu.make_async_copy(stage.at[t, s], out_ref.at[:, t * span + s], own_sem.at[s])

    def attend_unit(s, carry):
        for k in range(1, nt):
            forward(k, s).wait_recv()
        for i in range(nt):
            v = (recv[i, s].astype(jnp.float32) - mean) * gain + bias
            v = (v / (1.0 + jnp.exp(-v))).astype(jnp.bfloat16)
            normed_buf[:, i * frames:(i + 1) * frames] = v.reshape(cols, frames, channels)
        rows_in = normed_buf[...].reshape(cols * total, channels)
        qkv[...] = dot(rows_in, wqkv_ref[...]).astype(jnp.bfloat16).reshape(cols, total, 3 * channels)

        def scores_of(p):
            return lax.dot_general(
                split_pairs(qkv[p, :, channels:2 * channels]), split_within(qkv[p, :, 0:channels]),
                (((1,), (1,)), ((), ())), preferred_element_type=jnp.float32,
            ).reshape(pairs, total, within * total)

        def weights_of(value):
            top = jnp.max(value, axis=1, keepdims=True)
            parts = jnp.exp2((value - top) * factor)
            share = 1.0 / jnp.sum(parts, axis=1, keepdims=True)
            return (parts * share).astype(jnp.bfloat16).reshape(pairs * total, within * total)

        def mix(p, value):
            mixed = lax.dot_general(
                value, split_pairs(qkv[p, :, 2 * channels:]), (((0,), (0,)), ((), ())),
                preferred_element_type=jnp.float32,
            )
            result = mixed[0:total]
            for i in range(1, within):
                result = jnp.where(lane_head % within == i, mixed[i * total:(i + 1) * total], result)
            ctx[p] = result.astype(jnp.bfloat16)

        def pixel_group(g, inner):
            scores, weights = {}, {}
            for step in range(together + 2):
                if step < together:
                    scores[step] = scores_of(g * together + step)
                if 0 <= step - 1 < together:
                    weights[step - 1] = weights_of(scores.pop(step - 1))
                if 0 <= step - 2 < together:
                    mix(g * together + step - 2, weights.pop(step - 2))
            return inner

        lax.fori_loop(0, cols // together, pixel_group, 0)
        done = normed_buf[...].astype(jnp.float32).reshape(cols * total, channels)
        done = done + dot(ctx[...].reshape(cols * total, channels), wout_ref[...])
        for c in range(halves):
            turn_out[c] = done[:, c * lanes:(c + 1) * lanes]
        for i in range(nt):
            for f in range(frames):
                stage[i, s, f] = jnp.concatenate(
                    [turn_out[c, pl.ds(i * frames + f, cols, stride=total), :] for c in range(halves)],
                    axis=1,
                ).astype(jnp.bfloat16)
        for k in range(1, nt):
            back(k, s).start()
        own(s).start()
        return carry

    lax.fori_loop(0, span, attend_unit, 0)

    def drain(s, carry):
        own(s).wait()
        for k in range(1, nt):
            back(k, s).wait_recv()
            back(k, s).wait_send()
            forward(k, s).wait_send()
        return carry

    lax.fori_loop(0, span, drain, 0)
    for index, (dr, dc) in enumerate(STEPS):
        @pl.when(jnp.logical_and(inside(h + dr, nh), inside(w + dc, nw)))
        def _(index=index):
            halo(index, 1).wait_send()
    for side, step in ((0, -1), (1, 1)):
        @pl.when(inside(t + step, nt))
        def _(side=side):
            for s in range(span):
                edge(side, s, 1).wait_send()


def per_device(sizes, video, w_space, w_time, norm_gain, norm_bias, w_qkv, w_out):
    frames, rows, cols, channels = video.shape
    nt, nh, nw = sizes
    span = rows // nt
    unit = cols * frames
    total = nt * frames
    hbm = pl.BlockSpec(memory_space=pl.ANY)
    vmem = pl.BlockSpec(memory_space=pltpu.VMEM)
    bf16, f32, dma = jnp.bfloat16, jnp.float32, pltpu.SemaphoreType.DMA
    two = 2 if rows % 2 == 0 else 1
    pixels = rows * cols * frames
    lanes = math.gcd(channels, 128)
    halves = channels // lanes
    out = pl.pallas_call(
        functools.partial(kernel, sizes),
        out_shape=jax.ShapeDtypeStruct(video.shape, bf16),
        in_specs=[hbm] * 3 + [vmem] * 2 + [hbm] * 2,
        out_specs=hbm,
        scratch_shapes=[
            pltpu.VMEM(video.shape, bf16), pltpu.VMEM(w_space.shape, bf16), pltpu.VMEM(w_time.shape, bf16),
            pltpu.VMEM(w_qkv.shape, bf16), pltpu.VMEM(w_out.shape, bf16),
            pltpu.VMEM((rows + 2, cols + 2, frames, channels), bf16),
            pltpu.VMEM((rows, unit, channels), bf16),
            pltpu.VMEM((2, span, nt, cols, channels), bf16),
            pltpu.VMEM((2, span, nt, cols, channels), bf16),
            pltpu.VMEM((nt * halves, unit, lanes), f32),
            pltpu.VMEM((two * halves, unit, lanes), f32),
            pltpu.VMEM((halves, cols * total, lanes), f32),
            pltpu.VMEM((nt, span, unit, channels), bf16),
            pltpu.VMEM((nt, span, unit, channels), bf16),
            pltpu.VMEM((nt, span, frames, cols, channels), bf16),
            pltpu.VMEM((cols, total, 3 * channels), bf16),
            pltpu.VMEM((cols, total, channels), bf16),
            pltpu.VMEM((cols, total, channels), bf16),
            pltpu.VMEM((8, channels), f32),
            pltpu.VMEM((nt, 8, channels), f32),
            pltpu.VMEM((nh, 8, channels), f32),
            pltpu.VMEM((nw, 8, channels), f32),
            dma((5,)), dma((span,)), dma((len(STEPS),)), dma((len(STEPS),)), dma((2, span)), dma((2, span)),
            dma((nt, span)), dma((nt, span)), dma((nt, span)), dma((nt, span)),
            dma((nt,)), dma((nt,)), dma((nh,)), dma((nh,)), dma((nw,)), dma((nw,)),
        ],
        compiler_params=pltpu.CompilerParams(
            collective_id=0, has_side_effects=True, vmem_limit_bytes=60 * 1024 * 1024
        ),
        cost_estimate=pl.CostEstimate(
            flops=2 * pixels * channels * channels * 20,
            bytes_accessed=4 * pixels * channels, transcendentals=pixels * 64 * HEADS,
        ),
    )(
        video, w_space, w_time, norm_gain.reshape(1, channels), norm_bias.reshape(1, channels), w_qkv, w_out
    )
    return out


def solution(mesh):
    sizes = tuple(mesh.shape[name] for name in ("tm", "height", "width"))
    placed = (P("tm", "height", "width", None), P(), P(), P(), P(), P(), P())
    return jax.shard_map(
        functools.partial(per_device, sizes),
        mesh=mesh,
        in_specs=placed,
        out_specs=P("tm", "height", "width", None),
        check_vma=False,
    )
```

```python
import functools
import math

import jax
import jax.numpy as jnp
from jax import lax
from jax.experimental import pallas as pl
from jax.experimental.pallas import tpu as pltpu
from jax.sharding import PartitionSpec as P

HEADS = 8
GROUPS = 32
EPS = 1e-5
MESH = pl.DeviceIdType.MESH
STEPS = [(dr, dc) for dr in (-1, 0, 1) for dc in (-1, 0, 1) if (dr, dc) != (0, 0)]


def dot(a, b):
    return jnp.dot(a, b, preferred_element_type=jnp.float32)


def inside(index, size):
    return jnp.logical_and(index >= 0, index < size)


def kernel(
    sizes, x_hbm, wsp_hbm, wt_hbm, gain_ref, bias_ref, wqkv_hbm, wout_hbm, out_ref,
    x_ref, wsp_ref, wt_ref, wqkv_ref, wout_ref,
    pad, spat, edge_out, edge_in, tmp, turn, turn_out, piece, recv, stage, qkv, ctx, normed_buf,
    stat, ex_t, ex_h, ex_w,
    load_sem, own_sem, halo_send, halo_recv, edge_send, edge_recv, fwd_send, fwd_recv,
    back_send, back_recv, t_send, t_recv, h_send, h_recv, w_send, w_recv,
):
    nt, nh, nw = sizes
    frames, rows, cols, channels = x_ref.shape
    span = rows // nt
    unit = cols * frames
    total = nt * frames
    head = channels // HEADS
    t, h, w = (lax.axis_index(name) for name in ("tm", "height", "width"))

    barrier = pltpu.get_barrier_semaphore()
    count = 0
    for dr, dc in STEPS:
        there = jnp.logical_and(inside(h + dr, nh), inside(w + dc, nw))

        @pl.when(there)
        def _(dr=dr, dc=dc):
            pl.semaphore_signal(barrier, inc=1, device_id=(t, h + dr, w + dc), device_id_type=MESH)

        count = count + there.astype(jnp.int32)
    for k in range(1, nt):
        pl.semaphore_signal(barrier, inc=1, device_id=(lax.rem(t + k, nt), h, w), device_id_type=MESH)
    for k in range(1, nh):
        pl.semaphore_signal(barrier, inc=1, device_id=(t, lax.rem(h + k, nh), w), device_id_type=MESH)
    for k in range(1, nw):
        pl.semaphore_signal(barrier, inc=1, device_id=(t, h, lax.rem(w + k, nw)), device_id_type=MESH)

    loads = [
        pltpu.make_async_copy(src, dst, load_sem.at[i])
        for i, (src, dst) in enumerate((
            (x_hbm, x_ref), (wsp_hbm, wsp_ref), (wt_hbm, wt_ref), (wqkv_hbm, wqkv_ref), (wout_hbm, wout_ref),
        ))
    ]
    for load in loads:
        load.start()
    loads[0].wait()

    lanes = tmp.shape[2]
    halves = channels // lanes
    two = 2 if rows % 2 == 0 else 1

    def turn_in(step, carry):
        for b in range(two):
            r = step * two + b
            for c in range(halves):
                turn[b * halves + c] = x_ref[:, r, :, c * lanes:(c + 1) * lanes].astype(
                    jnp.float32
                ).reshape(unit, lanes)
            for i in range(cols):
                pad[r + 1, i + 1] = jnp.concatenate(
                    [turn[b * halves + c, pl.ds(i, frames, stride=cols), :] for c in range(halves)], axis=1
                ).astype(jnp.bfloat16)
        return carry

    lax.fori_loop(0, rows // two, turn_in, 0)
    pl.semaphore_wait(barrier, count + (nt - 1) + (nh - 1) + (nw - 1))

    def span_of(step, size):
        src = {-1: pl.ds(1, 1), 0: pl.ds(1, size), 1: pl.ds(size, 1)}[step]
        dst = {-1: pl.ds(size + 1, 1), 0: pl.ds(1, size), 1: pl.ds(0, 1)}[step]
        return src, dst

    def halo(index, sign):
        dr, dc = STEPS[index]
        (src_r, dst_r), (src_c, dst_c) = span_of(dr, rows), span_of(dc, cols)
        return pltpu.make_async_remote_copy(
            src_ref=pad.at[src_r, src_c], dst_ref=pad.at[dst_r, dst_c],
            send_sem=halo_send.at[index], recv_sem=halo_recv.at[index],
            device_id=(t, h + sign * dr, w + sign * dc), device_id_type=MESH,
        )

    for index, (dr, dc) in enumerate(STEPS):
        @pl.when(jnp.logical_and(inside(h + dr, nh), inside(w + dc, nw)))
        def _(index=index):
            halo(index, 1).start()
    for index, (dr, dc) in enumerate(STEPS):
        @pl.when(jnp.logical_not(jnp.logical_and(inside(h - dr, nh), inside(w - dc, nw))))
        def _(dr=dr, dc=dc):
            dst_r, dst_c = span_of(dr, rows)[1], span_of(dc, cols)[1]
            pad[dst_r, dst_c] = jnp.zeros((dst_r.size, dst_c.size, frames, channels), pad.dtype)
    for index, (dr, dc) in enumerate(STEPS):
        @pl.when(jnp.logical_and(inside(h - dr, nh), inside(w - dc, nw)))
        def _(index=index):
            halo(index, -1).wait_recv()

    block = 2 if nt % 2 == 0 else 1

    def edge(side, s, sign):
        step = (-1, 1)[side]
        return pltpu.make_async_remote_copy(
            src_ref=edge_out.at[side, s], dst_ref=edge_in.at[side, s],
            send_sem=edge_send.at[side, s], recv_sem=edge_recv.at[side, s],
            device_id=(t + sign * step, h, w), device_id_type=MESH,
        )

    def conv_round(s):
        for first in range(0, nt, block):
            acc = jnp.zeros((block * unit, channels), jnp.float32)
            for i in range(3):
                for j in range(3):
                    taps = jnp.concatenate(
                        [pad[(first + b) * span + s + i, pl.ds(j, cols)].reshape(unit, channels)
                         for b in range(block)], axis=0
                    )
                    acc = acc + dot(taps, wsp_ref[i, j])
            value = acc.astype(jnp.bfloat16)
            for b in range(block):
                k = first + b
                here = value[b * unit:(b + 1) * unit]
                spat[k * span + s] = here
                for c in range(halves):
                    tmp[k * halves + c] = here[:, c * lanes:(c + 1) * lanes].astype(jnp.float32)
                for side, frame in ((0, 0), (1, frames - 1)):
                    edge_out[side, s, k] = jnp.concatenate(
                        [tmp[k * halves + c, pl.ds(frame, cols, stride=frames), :] for c in range(halves)],
                        axis=1,
                    ).astype(jnp.bfloat16)
        for side, step in ((0, -1), (1, 1)):
            @pl.when(inside(t + step, nt))
            def _(side=side):
                edge(side, s, 1).start()

    for side, step in ((0, -1), (1, 1)):
        @pl.when(jnp.logical_not(inside(t - step, nt)))
        def _(side=side):
            edge_in[side] = jnp.zeros(edge_in.shape[1:], edge_in.dtype)

    stat[...] = jnp.zeros_like(stat)
    frame_of = lax.rem(lax.broadcasted_iota(jnp.int32, (block * unit, channels), 0), frames)

    def forward(k, s):
        to = lax.rem(t + k, nt)
        return pltpu.make_async_remote_copy(
            src_ref=piece.at[k, s], dst_ref=recv.at[t, s],
            send_sem=fwd_send.at[k, s], recv_sem=fwd_recv.at[k, s],
            device_id=(to, h, w), device_id_type=MESH,
        )

    def spread(v):
        return jnp.broadcast_to(v[:, None, :], (block * cols, frames, channels)).reshape(block * unit, channels)

    def time_round(s, send):
        for side, step in ((0, -1), (1, 1)):
            @pl.when(inside(t - step, nt))
            def _(side=side):
                edge(side, s, -1).wait_recv()
        order = list(range(1, nt)) + [0]
        for place in range(0, nt, block):
            ks = order[place:place + block]
            chunks = [lax.rem(t + k, nt) for k in ks]
            here = jnp.concatenate([spat[chunk * span + s] for chunk in chunks], axis=0)
            ends = [jnp.concatenate([edge_in[side, s, chunk] for chunk in chunks], axis=0) for side in (0, 1)]
            value = here.astype(jnp.float32) + dot(here, wt_ref[1])
            before = pltpu.roll(dot(here, wt_ref[0]), 1, 0)
            value = value + jnp.where(frame_of == 0, spread(dot(ends[1], wt_ref[0])), before)
            after = pltpu.roll(dot(here, wt_ref[2]), block * unit - 1, 0)
            value = value + jnp.where(frame_of == frames - 1, spread(dot(ends[0], wt_ref[2])), after)
            value = value.astype(jnp.bfloat16)
            for b, k in enumerate(ks):
                part = value[b * unit:(b + 1) * unit]
                if k:
                    piece[k, s] = part
                    if send:
                        forward(k, s).start()
                else:
                    recv[t, s] = part
            wide = value.astype(jnp.float32)
            stat[0:1] += jnp.sum(wide, axis=0, keepdims=True)
            stat[1:2] += jnp.sum(wide * wide, axis=0, keepdims=True)

    def both(s, carry):
        conv_round(s)
        time_round(s - 1, True)
        return carry

    for load in loads[1:]:
        load.wait()
    conv_round(0)
    lax.fori_loop(1, span, both, 0)
    time_round(span - 1, False)

    def exchange(slots, size, me, device, send, arrive, then=None):
        slots[me] = stat[...]

        def copy(k):
            return pltpu.make_async_remote_copy(
                src_ref=slots.at[me], dst_ref=slots.at[me],
                send_sem=send.at[k], recv_sem=arrive.at[k],
                device_id=device(lax.rem(me + k, size)), device_id_type=MESH,
            )

        def landed(k):
            other = lax.rem(me + size - k, size)
            return pltpu.make_async_remote_copy(
                src_ref=slots.at[other], dst_ref=slots.at[other],
                send_sem=send.at[k], recv_sem=arrive.at[k],
                device_id=device(other), device_id_type=MESH,
            )

        for k in range(1, size):
            copy(k).start()
        if then is not None:
            then()
        for k in range(1, size):
            landed(k).wait_recv()
        stat[...] = jnp.sum(slots[...], axis=0)
        for k in range(1, size):
            copy(k).wait_send()

    exchange(ex_h, nh, h, lambda o: (t, o, w), h_send, h_recv)
    exchange(ex_w, nw, w, lambda o: (t, h, o), w_send, w_recv)

    def send_last():
        for k in range(1, nt):
            forward(k, span - 1).start()

    exchange(ex_t, nt, t, lambda o: (o, h, w), t_send, t_recv, send_last)

    cells = float(total * rows * nh * cols * nw * (channels // GROUPS))
    size = channels // GROUPS
    same = (
        lax.broadcasted_iota(jnp.int32, (channels, channels), 0) // size
        == lax.broadcasted_iota(jnp.int32, (channels, channels), 1) // size
    ).astype(jnp.float32)
    sums = jnp.dot(
        stat[...], same, precision=lax.Precision.HIGHEST, preferred_element_type=jnp.float32
    ) / cells
    mean = sums[0:1]
    var = jnp.maximum(sums[1:2] - mean * mean, 0.0)
    gain = lax.rsqrt(var + EPS) * gain_ref[...]
    bias = bias_ref[...]

    lane_head = lax.broadcasted_iota(jnp.int32, (total, channels), 1) // head
    within = 2 if HEADS % 2 == 0 else 1
    pairs = HEADS // within
    together = math.gcd(cols, 8)

    def split_pairs(v):
        return jnp.concatenate(
            [jnp.where(lane_head // within == i, v, jnp.zeros_like(v)) for i in range(pairs)], axis=0
        )

    def split_within(v):
        return jnp.concatenate(
            [jnp.where(lane_head % within == i, v, jnp.zeros_like(v)) for i in range(within)], axis=0
        )

    factor = math.log2(math.e) / math.sqrt(head)

    def back(k, s):
        to = lax.rem(t + k, nt)
        return pltpu.make_async_remote_copy(
            src_ref=stage.at[to, s], dst_ref=out_ref.at[:, t * span + s],
            send_sem=back_send.at[k, s], recv_sem=back_recv.at[k, s],
            device_id=(to, h, w), device_id_type=MESH,
        )

    def own(s):
        return pltpu.make_async_copy(stage.at[t, s], out_ref.at[:, t * span + s], own_sem.at[s])

    def attend_unit(s, carry):
        for k in range(1, nt):
            forward(k, s).wait_recv()
        for i in range(nt):
            v = (recv[i, s].astype(jnp.float32) - mean) * gain + bias
            v = (v / (1.0 + jnp.exp(-v))).astype(jnp.bfloat16)
            normed_buf[:, i * frames:(i + 1) * frames] = v.reshape(cols, frames, channels)
        rows_in = normed_buf[...].reshape(cols * total, channels)
        qkv[...] = dot(rows_in, wqkv_ref[...]).astype(jnp.bfloat16).reshape(cols, total, 3 * channels)

        def scores_of(p):
            return lax.dot_general(
                split_pairs(qkv[p, :, channels:2 * channels]), split_within(qkv[p, :, 0:channels]),
                (((1,), (1,)), ((), ())), preferred_element_type=jnp.float32,
            ).reshape(pairs, total, within * total)

        def weights_of(value):
            top = jnp.max(value, axis=1, keepdims=True)
            parts = jnp.exp2((value - top) * factor)
            share = 1.0 / jnp.sum(parts, axis=1, keepdims=True)
            return (parts * share).astype(jnp.bfloat16).reshape(pairs * total, within * total)

        def mix(p, value):
            mixed = lax.dot_general(
                value, split_pairs(qkv[p, :, 2 * channels:]), (((0,), (0,)), ((), ())),
                preferred_element_type=jnp.float32,
            )
            result = mixed[0:total]
            for i in range(1, within):
                result = jnp.where(lane_head % within == i, mixed[i * total:(i + 1) * total], result)
            ctx[p] = result.astype(jnp.bfloat16)

        def pixel_group(g, inner):
            scores, weights = {}, {}
            for step in range(together + 2):
                if step < together:
                    scores[step] = scores_of(g * together + step)
                if 0 <= step - 1 < together:
                    weights[step - 1] = weights_of(scores.pop(step - 1))
                if 0 <= step - 2 < together:
                    mix(g * together + step - 2, weights.pop(step - 2))
            return inner

        lax.fori_loop(0, cols // together, pixel_group, 0)
        done = normed_buf[...].astype(jnp.float32).reshape(cols * total, channels)
        done = done + dot(ctx[...].reshape(cols * total, channels), wout_ref[...])
        for c in range(halves):
            turn_out[c] = done[:, c * lanes:(c + 1) * lanes]
        for i in range(nt):
            for f in range(frames):
                stage[i, s, f] = jnp.concatenate(
                    [turn_out[c, pl.ds(i * frames + f, cols, stride=total), :] for c in range(halves)],
                    axis=1,
                ).astype(jnp.bfloat16)
        for k in range(1, nt):
            back(k, s).start()
        own(s).start()
        return carry

    lax.fori_loop(0, span, attend_unit, 0)

    def drain(s, carry):
        own(s).wait()
        for k in range(1, nt):
            back(k, s).wait_recv()
            back(k, s).wait_send()
            forward(k, s).wait_send()
        return carry

    lax.fori_loop(0, span, drain, 0)
    for index, (dr, dc) in enumerate(STEPS):
        @pl.when(jnp.logical_and(inside(h + dr, nh), inside(w + dc, nw)))
        def _(index=index):
            halo(index, 1).wait_send()
    for side, step in ((0, -1), (1, 1)):
        @pl.when(inside(t + step, nt))
        def _(side=side):
            for s in range(span):
                edge(side, s, 1).wait_send()


def per_device(sizes, video, w_space, w_time, norm_gain, norm_bias, w_qkv, w_out):
    frames, rows, cols, channels = video.shape
    nt, nh, nw = sizes
    span = rows // nt
    unit = cols * frames
    total = nt * frames
    hbm = pl.BlockSpec(memory_space=pl.ANY)
    vmem = pl.BlockSpec(memory_space=pltpu.VMEM)
    bf16, f32, dma = jnp.bfloat16, jnp.float32, pltpu.SemaphoreType.DMA
    two = 2 if rows % 2 == 0 else 1
    pixels = rows * cols * frames
    lanes = math.gcd(channels, 128)
    halves = channels // lanes
    out = pl.pallas_call(
        functools.partial(kernel, sizes),
        out_shape=jax.ShapeDtypeStruct(video.shape, bf16),
        in_specs=[hbm] * 3 + [vmem] * 2 + [hbm] * 2,
        out_specs=hbm,
        scratch_shapes=[
            pltpu.VMEM(video.shape, bf16), pltpu.VMEM(w_space.shape, bf16), pltpu.VMEM(w_time.shape, bf16),
            pltpu.VMEM(w_qkv.shape, bf16), pltpu.VMEM(w_out.shape, bf16),
            pltpu.VMEM((rows + 2, cols + 2, frames, channels), bf16),
            pltpu.VMEM((rows, unit, channels), bf16),
            pltpu.VMEM((2, span, nt, cols, channels), bf16),
            pltpu.VMEM((2, span, nt, cols, channels), bf16),
            pltpu.VMEM((nt * halves, unit, lanes), f32),
            pltpu.VMEM((two * halves, unit, lanes), f32),
            pltpu.VMEM((halves, cols * total, lanes), f32),
            pltpu.VMEM((nt, span, unit, channels), bf16),
            pltpu.VMEM((nt, span, unit, channels), bf16),
            pltpu.VMEM((nt, span, frames, cols, channels), bf16),
            pltpu.VMEM((cols, total, 3 * channels), bf16),
            pltpu.VMEM((cols, total, channels), bf16),
            pltpu.VMEM((cols, total, channels), bf16),
            pltpu.VMEM((8, channels), f32),
            pltpu.VMEM((nt, 8, channels), f32),
            pltpu.VMEM((nh, 8, channels), f32),
            pltpu.VMEM((nw, 8, channels), f32),
            dma((5,)), dma((span,)), dma((len(STEPS),)), dma((len(STEPS),)), dma((2, span)), dma((2, span)),
            dma((nt, span)), dma((nt, span)), dma((nt, span)), dma((nt, span)),
            dma((nt,)), dma((nt,)), dma((nh,)), dma((nh,)), dma((nw,)), dma((nw,)),
        ],
        compiler_params=pltpu.CompilerParams(
            collective_id=0, has_side_effects=True, vmem_limit_bytes=60 * 1024 * 1024
        ),
        cost_estimate=pl.CostEstimate(
            flops=2 * pixels * channels * channels * 20,
            bytes_accessed=4 * pixels * channels, transcendentals=pixels * 64 * HEADS,
        ),
    )(
        video, w_space, w_time, norm_gain.reshape(1, channels), norm_bias.reshape(1, channels), w_qkv, w_out
    )
    return out


def solution(mesh):
    sizes = tuple(mesh.shape[name] for name in ("tm", "height", "width"))
    placed = (P("tm", "height", "width", None), P(), P(), P(), P(), P(), P())
    return jax.shard_map(
        functools.partial(per_device, sizes),
        mesh=mesh,
        in_specs=placed,
        out_specs=P("tm", "height", "width", None),
        check_vma=False,
    )
```

```python
import functools
import math

import jax
import jax.numpy as jnp
from jax import lax
from jax.experimental import pallas as pl
from jax.experimental.pallas import tpu as pltpu
from jax.sharding import PartitionSpec as P

HEADS = 8
GROUPS = 32
EPS = 1e-5
MESH = pl.DeviceIdType.MESH
STEPS = [(dr, dc) for dr in (-1, 0, 1) for dc in (-1, 0, 1) if (dr, dc) != (0, 0)]


def dot(a, b):
    return jnp.dot(a, b, preferred_element_type=jnp.float32)


def inside(index, size):
    return jnp.logical_and(index >= 0, index < size)


def kernel(
    sizes, x_hbm, wsp_hbm, wt_hbm, gain_ref, bias_ref, wqkv_hbm, wout_hbm, out_ref,
    x_ref, wsp_ref, wt_ref, wqkv_ref, wout_ref,
    pad, spat, edge_out, edge_in, tmp, turn, turn_out, piece, recv, stage, qkv, ctx, normed_buf,
    stat, ex_t, ex_h, ex_w,
    load_sem, own_sem, halo_send, halo_recv, edge_send, edge_recv, fwd_send, fwd_recv,
    back_send, back_recv, t_send, t_recv, h_send, h_recv, w_send, w_recv,
):
    nt, nh, nw = sizes
    frames, rows, cols, channels = x_ref.shape
    span = rows // nt
    unit = cols * frames
    total = nt * frames
    head = channels // HEADS
    t, h, w = (lax.axis_index(name) for name in ("tm", "height", "width"))

    barrier = pltpu.get_barrier_semaphore()
    count = 0
    for dr, dc in STEPS:
        there = jnp.logical_and(inside(h + dr, nh), inside(w + dc, nw))

        @pl.when(there)
        def _(dr=dr, dc=dc):
            pl.semaphore_signal(barrier, inc=1, device_id=(t, h + dr, w + dc), device_id_type=MESH)

        count = count + there.astype(jnp.int32)
    for k in range(1, nt):
        pl.semaphore_signal(barrier, inc=1, device_id=(lax.rem(t + k, nt), h, w), device_id_type=MESH)
    for k in range(1, nh):
        pl.semaphore_signal(barrier, inc=1, device_id=(t, lax.rem(h + k, nh), w), device_id_type=MESH)
    for k in range(1, nw):
        pl.semaphore_signal(barrier, inc=1, device_id=(t, h, lax.rem(w + k, nw)), device_id_type=MESH)

    loads = [
        pltpu.make_async_copy(src, dst, load_sem.at[i])
        for i, (src, dst) in enumerate((
            (x_hbm, x_ref), (wsp_hbm, wsp_ref), (wt_hbm, wt_ref), (wqkv_hbm, wqkv_ref), (wout_hbm, wout_ref),
        ))
    ]
    for load in loads:
        load.start()
    loads[0].wait()

    lanes = tmp.shape[2]
    halves = channels // lanes
    two = 2 if rows % 2 == 0 else 1

    def turn_in(step, carry):
        for b in range(two):
            r = step * two + b
            for c in range(halves):
                turn[b * halves + c] = x_ref[:, r, :, c * lanes:(c + 1) * lanes].astype(
                    jnp.float32
                ).reshape(unit, lanes)
            for i in range(cols):
                pad[r + 1, i + 1] = jnp.concatenate(
                    [turn[b * halves + c, pl.ds(i, frames, stride=cols), :] for c in range(halves)], axis=1
                ).astype(jnp.bfloat16)
        return carry

    ends = sorted({0, rows // two - 1})
    for step in ends:
        turn_in(step, 0)
    pl.semaphore_wait(barrier, count + (nt - 1) + (nh - 1) + (nw - 1))

    def span_of(step, size):
        src = {-1: pl.ds(1, 1), 0: pl.ds(1, size), 1: pl.ds(size, 1)}[step]
        dst = {-1: pl.ds(size + 1, 1), 0: pl.ds(1, size), 1: pl.ds(0, 1)}[step]
        return src, dst

    def halo(index, sign):
        dr, dc = STEPS[index]
        (src_r, dst_r), (src_c, dst_c) = span_of(dr, rows), span_of(dc, cols)
        return pltpu.make_async_remote_copy(
            src_ref=pad.at[src_r, src_c], dst_ref=pad.at[dst_r, dst_c],
            send_sem=halo_send.at[index], recv_sem=halo_recv.at[index],
            device_id=(t, h + sign * dr, w + sign * dc), device_id_type=MESH,
        )

    def send_halos(along):
        for index, (dr, dc) in enumerate(STEPS):
            if (dr != 0) == along:
                @pl.when(jnp.logical_and(inside(h + dr, nh), inside(w + dc, nw)))
                def _(index=index):
                    halo(index, 1).start()

    send_halos(True)
    lax.fori_loop(1, rows // two - 1, turn_in, 0)
    send_halos(False)
    for index, (dr, dc) in enumerate(STEPS):
        @pl.when(jnp.logical_not(jnp.logical_and(inside(h - dr, nh), inside(w - dc, nw))))
        def _(dr=dr, dc=dc):
            dst_r, dst_c = span_of(dr, rows)[1], span_of(dc, cols)[1]
            pad[dst_r, dst_c] = jnp.zeros((dst_r.size, dst_c.size, frames, channels), pad.dtype)
    for index, (dr, dc) in enumerate(STEPS):
        @pl.when(jnp.logical_and(inside(h - dr, nh), inside(w - dc, nw)))
        def _(index=index):
            halo(index, -1).wait_recv()

    block = 2 if nt % 2 == 0 else 1

    def edge(side, s, sign):
        step = (-1, 1)[side]
        return pltpu.make_async_remote_copy(
            src_ref=edge_out.at[side, s], dst_ref=edge_in.at[side, s],
            send_sem=edge_send.at[side, s], recv_sem=edge_recv.at[side, s],
            device_id=(t + sign * step, h, w), device_id_type=MESH,
        )

    def conv_round(s):
        for first in range(0, nt, block):
            acc = jnp.zeros((block * unit, channels), jnp.float32)
            for i in range(3):
                for j in range(3):
                    taps = jnp.concatenate(
                        [pad[(first + b) * span + s + i, pl.ds(j, cols)].reshape(unit, channels)
                         for b in range(block)], axis=0
                    )
                    acc = acc + dot(taps, wsp_ref[i, j])
            value = acc.astype(jnp.bfloat16)
            for b in range(block):
                k = first + b
                here = value[b * unit:(b + 1) * unit]
                spat[k * span + s] = here
                for c in range(halves):
                    tmp[k * halves + c] = here[:, c * lanes:(c + 1) * lanes].astype(jnp.float32)
                for side, frame in ((0, 0), (1, frames - 1)):
                    edge_out[side, s, k] = jnp.concatenate(
                        [tmp[k * halves + c, pl.ds(frame, cols, stride=frames), :] for c in range(halves)],
                        axis=1,
                    ).astype(jnp.bfloat16)
        for side, step in ((0, -1), (1, 1)):
            @pl.when(inside(t + step, nt))
            def _(side=side):
                edge(side, s, 1).start()

    for side, step in ((0, -1), (1, 1)):
        @pl.when(jnp.logical_not(inside(t - step, nt)))
        def _(side=side):
            edge_in[side] = jnp.zeros(edge_in.shape[1:], edge_in.dtype)

    stat[...] = jnp.zeros_like(stat)
    frame_of = lax.rem(lax.broadcasted_iota(jnp.int32, (block * unit, channels), 0), frames)

    def forward(k, s):
        to = lax.rem(t + k, nt)
        return pltpu.make_async_remote_copy(
            src_ref=piece.at[k, s], dst_ref=recv.at[t, s],
            send_sem=fwd_send.at[k, s], recv_sem=fwd_recv.at[k, s],
            device_id=(to, h, w), device_id_type=MESH,
        )

    def spread(v):
        return jnp.broadcast_to(v[:, None, :], (block * cols, frames, channels)).reshape(block * unit, channels)

    def time_round(s, send):
        for side, step in ((0, -1), (1, 1)):
            @pl.when(inside(t - step, nt))
            def _(side=side):
                edge(side, s, -1).wait_recv()
        order = list(range(1, nt)) + [0]
        for place in range(0, nt, block):
            ks = order[place:place + block]
            chunks = [lax.rem(t + k, nt) for k in ks]
            here = jnp.concatenate([spat[chunk * span + s] for chunk in chunks], axis=0)
            ends = [jnp.concatenate([edge_in[side, s, chunk] for chunk in chunks], axis=0) for side in (0, 1)]
            value = here.astype(jnp.float32) + dot(here, wt_ref[1])
            before = pltpu.roll(dot(here, wt_ref[0]), 1, 0)
            value = value + jnp.where(frame_of == 0, spread(dot(ends[1], wt_ref[0])), before)
            after = pltpu.roll(dot(here, wt_ref[2]), block * unit - 1, 0)
            value = value + jnp.where(frame_of == frames - 1, spread(dot(ends[0], wt_ref[2])), after)
            value = value.astype(jnp.bfloat16)
            for b, k in enumerate(ks):
                part = value[b * unit:(b + 1) * unit]
                if k:
                    piece[k, s] = part
                    if send:
                        forward(k, s).start()
                else:
                    recv[t, s] = part
            wide = value.astype(jnp.float32)
            stat[0:1] += jnp.sum(wide, axis=0, keepdims=True)
            stat[1:2] += jnp.sum(wide * wide, axis=0, keepdims=True)

    def both(s, carry):
        conv_round(s)
        time_round(s - 1, True)
        return carry

    for load in loads[1:]:
        load.wait()
    conv_round(0)
    lax.fori_loop(1, span, both, 0)
    time_round(span - 1, False)

    def exchange(slots, size, me, device, send, arrive, then=None):
        slots[me] = stat[...]

        def copy(k):
            return pltpu.make_async_remote_copy(
                src_ref=slots.at[me], dst_ref=slots.at[me],
                send_sem=send.at[k], recv_sem=arrive.at[k],
                device_id=device(lax.rem(me + k, size)), device_id_type=MESH,
            )

        def landed(k):
            other = lax.rem(me + size - k, size)
            return pltpu.make_async_remote_copy(
                src_ref=slots.at[other], dst_ref=slots.at[other],
                send_sem=send.at[k], recv_sem=arrive.at[k],
                device_id=device(other), device_id_type=MESH,
            )

        for k in range(1, size):
            copy(k).start()
        if then is not None:
            then()
        for k in range(1, size):
            landed(k).wait_recv()
        stat[...] = jnp.sum(slots[...], axis=0)
        for k in range(1, size):
            copy(k).wait_send()

    exchange(ex_h, nh, h, lambda o: (t, o, w), h_send, h_recv)
    exchange(ex_w, nw, w, lambda o: (t, h, o), w_send, w_recv)

    def send_last():
        for k in range(1, nt):
            forward(k, span - 1).start()

    exchange(ex_t, nt, t, lambda o: (o, h, w), t_send, t_recv, send_last)

    cells = float(total * rows * nh * cols * nw * (channels // GROUPS))
    size = channels // GROUPS
    same = (
        lax.broadcasted_iota(jnp.int32, (channels, channels), 0) // size
        == lax.broadcasted_iota(jnp.int32, (channels, channels), 1) // size
    ).astype(jnp.float32)
    sums = jnp.dot(
        stat[...], same, precision=lax.Precision.HIGHEST, preferred_element_type=jnp.float32
    ) / cells
    mean = sums[0:1]
    var = jnp.maximum(sums[1:2] - mean * mean, 0.0)
    gain = lax.rsqrt(var + EPS) * gain_ref[...]
    bias = bias_ref[...]

    lane_head = lax.broadcasted_iota(jnp.int32, (total, channels), 1) // head
    within = 2 if HEADS % 2 == 0 else 1
    pairs = HEADS // within
    together = math.gcd(cols, 8)

    def split_pairs(v):
        return jnp.concatenate(
            [jnp.where(lane_head // within == i, v, jnp.zeros_like(v)) for i in range(pairs)], axis=0
        )

    def split_within(v):
        return jnp.concatenate(
            [jnp.where(lane_head % within == i, v, jnp.zeros_like(v)) for i in range(within)], axis=0
        )

    factor = math.log2(math.e) / math.sqrt(head)

    def back(k, s):
        to = lax.rem(t + k, nt)
        return pltpu.make_async_remote_copy(
            src_ref=stage.at[to, s], dst_ref=out_ref.at[:, t * span + s],
            send_sem=back_send.at[k, s], recv_sem=back_recv.at[k, s],
            device_id=(to, h, w), device_id_type=MESH,
        )

    def own(s):
        return pltpu.make_async_copy(stage.at[t, s], out_ref.at[:, t * span + s], own_sem.at[s])

    def attend_unit(s, carry):
        for k in range(1, nt):
            forward(k, s).wait_recv()
        for i in range(nt):
            v = (recv[i, s].astype(jnp.float32) - mean) * gain + bias
            v = (v / (1.0 + jnp.exp(-v))).astype(jnp.bfloat16)
            normed_buf[:, i * frames:(i + 1) * frames] = v.reshape(cols, frames, channels)
        rows_in = normed_buf[...].reshape(cols * total, channels)
        qkv[...] = dot(rows_in, wqkv_ref[...]).astype(jnp.bfloat16).reshape(cols, total, 3 * channels)

        def scores_of(p):
            return lax.dot_general(
                split_pairs(qkv[p, :, channels:2 * channels]), split_within(qkv[p, :, 0:channels]),
                (((1,), (1,)), ((), ())), preferred_element_type=jnp.float32,
            ).reshape(pairs, total, within * total)

        def weights_of(value):
            top = jnp.max(value, axis=1, keepdims=True)
            parts = jnp.exp2((value - top) * factor)
            share = 1.0 / jnp.sum(parts, axis=1, keepdims=True)
            return (parts * share).astype(jnp.bfloat16).reshape(pairs * total, within * total)

        def mix(p, value):
            mixed = lax.dot_general(
                value, split_pairs(qkv[p, :, 2 * channels:]), (((0,), (0,)), ((), ())),
                preferred_element_type=jnp.float32,
            )
            result = mixed[0:total]
            for i in range(1, within):
                result = jnp.where(lane_head % within == i, mixed[i * total:(i + 1) * total], result)
            ctx[p] = result.astype(jnp.bfloat16)

        def pixel_group(g, inner):
            scores, weights = {}, {}
            for step in range(together + 2):
                if step < together:
                    scores[step] = scores_of(g * together + step)
                if 0 <= step - 1 < together:
                    weights[step - 1] = weights_of(scores.pop(step - 1))
                if 0 <= step - 2 < together:
                    mix(g * together + step - 2, weights.pop(step - 2))
            return inner

        lax.fori_loop(0, cols // together, pixel_group, 0)
        done = normed_buf[...].astype(jnp.float32).reshape(cols * total, channels)
        done = done + dot(ctx[...].reshape(cols * total, channels), wout_ref[...])
        for c in range(halves):
            turn_out[c] = done[:, c * lanes:(c + 1) * lanes]
        for i in range(nt):
            for f in range(frames):
                stage[i, s, f] = jnp.concatenate(
                    [turn_out[c, pl.ds(i * frames + f, cols, stride=total), :] for c in range(halves)],
                    axis=1,
                ).astype(jnp.bfloat16)
        for k in range(1, nt):
            back(k, s).start()
        own(s).start()
        return carry

    lax.fori_loop(0, span, attend_unit, 0)

    def drain(s, carry):
        own(s).wait()
        for k in range(1, nt):
            back(k, s).wait_recv()
            back(k, s).wait_send()
            forward(k, s).wait_send()
        return carry

    lax.fori_loop(0, span, drain, 0)
    for index, (dr, dc) in enumerate(STEPS):
        @pl.when(jnp.logical_and(inside(h + dr, nh), inside(w + dc, nw)))
        def _(index=index):
            halo(index, 1).wait_send()
    for side, step in ((0, -1), (1, 1)):
        @pl.when(inside(t + step, nt))
        def _(side=side):
            for s in range(span):
                edge(side, s, 1).wait_send()


def copy_kernel(src_ref, dst_ref):
    dst_ref[...] = src_ref[...]


def per_device(sizes, video, w_space, w_time, norm_gain, norm_bias, w_qkv, w_out):
    frames, rows, cols, channels = video.shape
    nt, nh, nw = sizes
    span = rows // nt
    unit = cols * frames
    total = nt * frames
    hbm = pl.BlockSpec(memory_space=pl.ANY)
    vmem = pl.BlockSpec(memory_space=pltpu.VMEM)
    bf16, f32, dma = jnp.bfloat16, jnp.float32, pltpu.SemaphoreType.DMA
    two = 2 if rows % 2 == 0 else 1
    pixels = rows * cols * frames
    lanes = math.gcd(channels, 128)
    halves = channels // lanes
    out = pl.pallas_call(
        functools.partial(kernel, sizes),
        out_shape=jax.ShapeDtypeStruct(video.shape, bf16),
        in_specs=[hbm] * 3 + [vmem] * 2 + [hbm] * 2,
        out_specs=hbm,
        scratch_shapes=[
            pltpu.VMEM(video.shape, bf16), pltpu.VMEM(w_space.shape, bf16), pltpu.VMEM(w_time.shape, bf16),
            pltpu.VMEM(w_qkv.shape, bf16), pltpu.VMEM(w_out.shape, bf16),
            pltpu.VMEM((rows + 2, cols + 2, frames, channels), bf16),
            pltpu.VMEM((rows, unit, channels), bf16),
            pltpu.VMEM((2, span, nt, cols, channels), bf16),
            pltpu.VMEM((2, span, nt, cols, channels), bf16),
            pltpu.VMEM((nt * halves, unit, lanes), f32),
            pltpu.VMEM((two * halves, unit, lanes), f32),
            pltpu.VMEM((halves, cols * total, lanes), f32),
            pltpu.VMEM((nt, span, unit, channels), bf16),
            pltpu.VMEM((nt, span, unit, channels), bf16),
            pltpu.VMEM((nt, span, frames, cols, channels), bf16),
            pltpu.VMEM((cols, total, 3 * channels), bf16),
            pltpu.VMEM((cols, total, channels), bf16),
            pltpu.VMEM((cols, total, channels), bf16),
            pltpu.VMEM((8, channels), f32),
            pltpu.VMEM((nt, 8, channels), f32),
            pltpu.VMEM((nh, 8, channels), f32),
            pltpu.VMEM((nw, 8, channels), f32),
            dma((5,)), dma((span,)), dma((len(STEPS),)), dma((len(STEPS),)), dma((2, span)), dma((2, span)),
            dma((nt, span)), dma((nt, span)), dma((nt, span)), dma((nt, span)),
            dma((nt,)), dma((nt,)), dma((nh,)), dma((nh,)), dma((nw,)), dma((nw,)),
        ],
        compiler_params=pltpu.CompilerParams(
            collective_id=0, has_side_effects=True, vmem_limit_bytes=60 * 1024 * 1024
        ),
        cost_estimate=pl.CostEstimate(
            flops=2 * pixels * channels * channels * 20,
            bytes_accessed=4 * pixels * channels, transcendentals=pixels * 64 * HEADS,
        ),
    )(
        video, w_space, w_time, norm_gain.reshape(1, channels), norm_bias.reshape(1, channels), w_qkv, w_out
    )
    part = frames // math.gcd(frames, 4)
    block = pl.BlockSpec((part, rows, cols, channels), lambda i: (i, 0, 0, 0))
    return pl.pallas_call(
        copy_kernel,
        out_shape=jax.ShapeDtypeStruct(video.shape, bf16),
        grid=(frames // part,),
        in_specs=[block],
        out_specs=block,
    )(out)


def solution(mesh):
    sizes = tuple(mesh.shape[name] for name in ("tm", "height", "width"))
    placed = (P("tm", "height", "width", None), P(), P(), P(), P(), P(), P())
    return jax.shard_map(
        functools.partial(per_device, sizes),
        mesh=mesh,
        in_specs=placed,
        out_specs=P("tm", "height", "width", None),
        check_vma=False,
    )
```

```python
import functools
import math

import jax
import jax.numpy as jnp
from jax import lax
from jax.experimental import pallas as pl
from jax.experimental.pallas import tpu as pltpu
from jax.sharding import PartitionSpec as P

HEADS = 8
GROUPS = 32
EPS = 1e-5
MESH = pl.DeviceIdType.MESH
STEPS = [(dr, dc) for dr in (-1, 0, 1) for dc in (-1, 0, 1) if (dr, dc) != (0, 0)]


def dot(a, b):
    return jnp.dot(a, b, preferred_element_type=jnp.float32)


def inside(index, size):
    return jnp.logical_and(index >= 0, index < size)


def kernel(
    sizes, x_hbm, wsp_hbm, wt_hbm, gain_ref, bias_ref, wqkv_hbm, wout_hbm, out_ref,
    x_ref, wsp_ref, wt_ref, wqkv_ref, wout_ref,
    pad, spat, edge_out, edge_in, tmp, turn, turn_out, piece, recv, stage, qkv, ctx, normed_buf,
    stat, ex_t, ex_h, ex_w,
    load_sem, own_sem, halo_send, halo_recv, edge_send, edge_recv, fwd_send, fwd_recv,
    back_send, back_recv, t_send, t_recv, h_send, h_recv, w_send, w_recv,
):
    nt, nh, nw = sizes
    frames, rows, cols, channels = x_ref.shape
    span = rows // nt
    unit = cols * frames
    total = nt * frames
    head = channels // HEADS
    t, h, w = (lax.axis_index(name) for name in ("tm", "height", "width"))

    barrier = pltpu.get_barrier_semaphore()
    count = 0
    for dr, dc in STEPS:
        there = jnp.logical_and(inside(h + dr, nh), inside(w + dc, nw))

        @pl.when(there)
        def _(dr=dr, dc=dc):
            pl.semaphore_signal(barrier, inc=1, device_id=(t, h + dr, w + dc), device_id_type=MESH)

        count = count + there.astype(jnp.int32)
    for k in range(1, nt):
        pl.semaphore_signal(barrier, inc=1, device_id=(lax.rem(t + k, nt), h, w), device_id_type=MESH)
    for k in range(1, nh):
        pl.semaphore_signal(barrier, inc=1, device_id=(t, lax.rem(h + k, nh), w), device_id_type=MESH)
    for k in range(1, nw):
        pl.semaphore_signal(barrier, inc=1, device_id=(t, h, lax.rem(w + k, nw)), device_id_type=MESH)

    loads = [
        pltpu.make_async_copy(src, dst, load_sem.at[i])
        for i, (src, dst) in enumerate((
            (x_hbm, x_ref), (wsp_hbm, wsp_ref), (wt_hbm, wt_ref), (wqkv_hbm, wqkv_ref), (wout_hbm, wout_ref),
        ))
    ]
    for load in loads:
        load.start()
    loads[0].wait()

    lanes = tmp.shape[2]
    halves = channels // lanes
    two = 2 if rows % 2 == 0 else 1

    def turn_in(step, carry):
        for b in range(two):
            r = step * two + b
            for c in range(halves):
                turn[b * halves + c] = x_ref[:, r, :, c * lanes:(c + 1) * lanes].astype(
                    jnp.float32
                ).reshape(unit, lanes)
            for i in range(cols):
                pad[r + 1, i + 1] = jnp.concatenate(
                    [turn[b * halves + c, pl.ds(i, frames, stride=cols), :] for c in range(halves)], axis=1
                ).astype(jnp.bfloat16)
        return carry

    ends = sorted({0, rows // two - 1})
    for step in ends:
        turn_in(step, 0)
    pl.semaphore_wait(barrier, count + (nt - 1) + (nh - 1) + (nw - 1))

    def span_of(step, size):
        src = {-1: pl.ds(1, 1), 0: pl.ds(1, size), 1: pl.ds(size, 1)}[step]
        dst = {-1: pl.ds(size + 1, 1), 0: pl.ds(1, size), 1: pl.ds(0, 1)}[step]
        return src, dst

    def halo(index, sign):
        dr, dc = STEPS[index]
        (src_r, dst_r), (src_c, dst_c) = span_of(dr, rows), span_of(dc, cols)
        return pltpu.make_async_remote_copy(
            src_ref=pad.at[src_r, src_c], dst_ref=pad.at[dst_r, dst_c],
            send_sem=halo_send.at[index], recv_sem=halo_recv.at[index],
            device_id=(t, h + sign * dr, w + sign * dc), device_id_type=MESH,
        )

    def send_halos(along):
        for index, (dr, dc) in enumerate(STEPS):
            if (dr != 0) == along:
                @pl.when(jnp.logical_and(inside(h + dr, nh), inside(w + dc, nw)))
                def _(index=index):
                    halo(index, 1).start()

    send_halos(True)
    lax.fori_loop(1, rows // two - 1, turn_in, 0)
    send_halos(False)
    for index, (dr, dc) in enumerate(STEPS):
        @pl.when(jnp.logical_not(jnp.logical_and(inside(h - dr, nh), inside(w - dc, nw))))
        def _(dr=dr, dc=dc):
            dst_r, dst_c = span_of(dr, rows)[1], span_of(dc, cols)[1]
            pad[dst_r, dst_c] = jnp.zeros((dst_r.size, dst_c.size, frames, channels), pad.dtype)
    for index, (dr, dc) in enumerate(STEPS):
        @pl.when(jnp.logical_and(inside(h - dr, nh), inside(w - dc, nw)))
        def _(index=index):
            halo(index, -1).wait_recv()

    block = 2 if nt % 2 == 0 else 1

    def edge(side, s, sign):
        step = (-1, 1)[side]
        return pltpu.make_async_remote_copy(
            src_ref=edge_out.at[side, s], dst_ref=edge_in.at[side, s],
            send_sem=edge_send.at[side, s], recv_sem=edge_recv.at[side, s],
            device_id=(t + sign * step, h, w), device_id_type=MESH,
        )

    def conv_round(s):
        for first in range(0, nt, block):
            acc = jnp.zeros((block * unit, channels), jnp.float32)
            for i in range(3):
                for j in range(3):
                    taps = jnp.concatenate(
                        [pad[(first + b) * span + s + i, pl.ds(j, cols)].reshape(unit, channels)
                         for b in range(block)], axis=0
                    )
                    acc = acc + dot(taps, wsp_ref[i, j])
            value = acc.astype(jnp.bfloat16)
            for b in range(block):
                k = first + b
                here = value[b * unit:(b + 1) * unit]
                spat[k * span + s] = here
                for c in range(halves):
                    tmp[k * halves + c] = here[:, c * lanes:(c + 1) * lanes].astype(jnp.float32)
                for side, frame in ((0, 0), (1, frames - 1)):
                    edge_out[side, s, k] = jnp.concatenate(
                        [tmp[k * halves + c, pl.ds(frame, cols, stride=frames), :] for c in range(halves)],
                        axis=1,
                    ).astype(jnp.bfloat16)
        for side, step in ((0, -1), (1, 1)):
            @pl.when(inside(t + step, nt))
            def _(side=side):
                edge(side, s, 1).start()

    for side, step in ((0, -1), (1, 1)):
        @pl.when(jnp.logical_not(inside(t - step, nt)))
        def _(side=side):
            edge_in[side] = jnp.zeros(edge_in.shape[1:], edge_in.dtype)

    stat[...] = jnp.zeros_like(stat)
    frame_of = lax.rem(lax.broadcasted_iota(jnp.int32, (block * unit, channels), 0), frames)

    def forward(k, s):
        to = lax.rem(t + k, nt)
        return pltpu.make_async_remote_copy(
            src_ref=piece.at[k, s], dst_ref=recv.at[t, s],
            send_sem=fwd_send.at[k, s], recv_sem=fwd_recv.at[k, s],
            device_id=(to, h, w), device_id_type=MESH,
        )

    def spread(v):
        return jnp.broadcast_to(v[:, None, :], (block * cols, frames, channels)).reshape(block * unit, channels)

    def time_round(s, send):
        for side, step in ((0, -1), (1, 1)):
            @pl.when(inside(t - step, nt))
            def _(side=side):
                edge(side, s, -1).wait_recv()
        order = list(range(1, nt)) + [0]
        for place in range(0, nt, block):
            ks = order[place:place + block]
            chunks = [lax.rem(t + k, nt) for k in ks]
            here = jnp.concatenate([spat[chunk * span + s] for chunk in chunks], axis=0)
            ends = [jnp.concatenate([edge_in[side, s, chunk] for chunk in chunks], axis=0) for side in (0, 1)]
            value = here.astype(jnp.float32) + dot(here, wt_ref[1])
            before = pltpu.roll(dot(here, wt_ref[0]), 1, 0)
            value = value + jnp.where(frame_of == 0, spread(dot(ends[1], wt_ref[0])), before)
            after = pltpu.roll(dot(here, wt_ref[2]), block * unit - 1, 0)
            value = value + jnp.where(frame_of == frames - 1, spread(dot(ends[0], wt_ref[2])), after)
            value = value.astype(jnp.bfloat16)
            for b, k in enumerate(ks):
                part = value[b * unit:(b + 1) * unit]
                if k:
                    piece[k, s] = part
                    if send:
                        forward(k, s).start()
                else:
                    recv[t, s] = part
            wide = value.astype(jnp.float32)
            stat[0:1] += jnp.sum(wide, axis=0, keepdims=True)
            stat[1:2] += jnp.sum(wide * wide, axis=0, keepdims=True)

    def both(s, carry):
        conv_round(s)
        time_round(s - 1, True)
        return carry

    for load in loads[1:]:
        load.wait()
    conv_round(0)
    lax.fori_loop(1, span, both, 0)
    time_round(span - 1, False)

    def exchange(slots, size, me, device, send, arrive, then=None):
        slots[me] = stat[...]

        def copy(k):
            return pltpu.make_async_remote_copy(
                src_ref=slots.at[me], dst_ref=slots.at[me],
                send_sem=send.at[k], recv_sem=arrive.at[k],
                device_id=device(lax.rem(me + k, size)), device_id_type=MESH,
            )

        def landed(k):
            other = lax.rem(me + size - k, size)
            return pltpu.make_async_remote_copy(
                src_ref=slots.at[other], dst_ref=slots.at[other],
                send_sem=send.at[k], recv_sem=arrive.at[k],
                device_id=device(other), device_id_type=MESH,
            )

        for k in range(1, size):
            copy(k).start()
        if then is not None:
            then()
        for k in range(1, size):
            landed(k).wait_recv()
        stat[...] = jnp.sum(slots[...], axis=0)
        for k in range(1, size):
            copy(k).wait_send()

    exchange(ex_h, nh, h, lambda o: (t, o, w), h_send, h_recv)
    exchange(ex_w, nw, w, lambda o: (t, h, o), w_send, w_recv)

    def send_last():
        for k in range(1, nt):
            forward(k, span - 1).start()

    exchange(ex_t, nt, t, lambda o: (o, h, w), t_send, t_recv, send_last)

    cells = float(total * rows * nh * cols * nw * (channels // GROUPS))
    size = channels // GROUPS
    same = (
        lax.broadcasted_iota(jnp.int32, (channels, channels), 0) // size
        == lax.broadcasted_iota(jnp.int32, (channels, channels), 1) // size
    ).astype(jnp.float32)
    sums = jnp.dot(
        stat[...], same, precision=lax.Precision.HIGHEST, preferred_element_type=jnp.float32
    ) / cells
    mean = sums[0:1]
    var = jnp.maximum(sums[1:2] - mean * mean, 0.0)
    gain = lax.rsqrt(var + EPS) * gain_ref[...]
    bias = bias_ref[...]

    lane_head = lax.broadcasted_iota(jnp.int32, (total, channels), 1) // head
    within = 2 if HEADS % 2 == 0 else 1
    pairs = HEADS // within
    together = math.gcd(cols, 8)

    def split_pairs(v):
        return jnp.concatenate(
            [jnp.where(lane_head // within == i, v, jnp.zeros_like(v)) for i in range(pairs)], axis=0
        )

    def split_within(v):
        return jnp.concatenate(
            [jnp.where(lane_head % within == i, v, jnp.zeros_like(v)) for i in range(within)], axis=0
        )

    factor = math.log2(math.e) / math.sqrt(head)

    def back(k, s):
        to = lax.rem(t + k, nt)
        return pltpu.make_async_remote_copy(
            src_ref=stage.at[to, s], dst_ref=out_ref.at[:, t * span + s],
            send_sem=back_send.at[k, s], recv_sem=back_recv.at[k, s],
            device_id=(to, h, w), device_id_type=MESH,
        )

    def own(s):
        return pltpu.make_async_copy(stage.at[t, s], out_ref.at[:, t * span + s], own_sem.at[s])

    def attend_unit(s, carry):
        for k in range(1, nt):
            forward(k, s).wait_recv()
        for i in range(nt):
            v = (recv[i, s].astype(jnp.float32) - mean) * gain + bias
            v = (v / (1.0 + jnp.exp(-v))).astype(jnp.bfloat16)
            normed_buf[:, i * frames:(i + 1) * frames] = v.reshape(cols, frames, channels)
        rows_in = normed_buf[...].reshape(cols * total, channels)
        qkv[...] = dot(rows_in, wqkv_ref[...]).astype(jnp.bfloat16).reshape(cols, total, 3 * channels)

        def scores_of(p):
            return lax.dot_general(
                split_pairs(qkv[p, :, channels:2 * channels]), split_within(qkv[p, :, 0:channels]),
                (((1,), (1,)), ((), ())), preferred_element_type=jnp.float32,
            ).reshape(pairs, total, within * total)

        def weights_of(value):
            top = jnp.max(value, axis=1, keepdims=True)
            parts = jnp.exp2((value - top) * factor)
            share = 1.0 / jnp.sum(parts, axis=1, keepdims=True)
            return (parts * share).astype(jnp.bfloat16).reshape(pairs * total, within * total)

        def mix(p, value):
            mixed = lax.dot_general(
                value, split_pairs(qkv[p, :, 2 * channels:]), (((0,), (0,)), ((), ())),
                preferred_element_type=jnp.float32,
            )
            result = mixed[0:total]
            for i in range(1, within):
                result = jnp.where(lane_head % within == i, mixed[i * total:(i + 1) * total], result)
            ctx[p] = result.astype(jnp.bfloat16)

        def pixel_group(g, inner):
            scores, weights = {}, {}
            for step in range(together + 2):
                if step < together:
                    scores[step] = scores_of(g * together + step)
                if 0 <= step - 1 < together:
                    weights[step - 1] = weights_of(scores.pop(step - 1))
                if 0 <= step - 2 < together:
                    mix(g * together + step - 2, weights.pop(step - 2))
            return inner

        lax.fori_loop(0, cols // together, pixel_group, 0)
        done = normed_buf[...].astype(jnp.float32).reshape(cols * total, channels)
        done = done + dot(ctx[...].reshape(cols * total, channels), wout_ref[...])
        for c in range(halves):
            turn_out[c] = done[:, c * lanes:(c + 1) * lanes]
        for i in range(nt):
            for f in range(frames):
                stage[i, s, f] = jnp.concatenate(
                    [turn_out[c, pl.ds(i * frames + f, cols, stride=total), :] for c in range(halves)],
                    axis=1,
                ).astype(jnp.bfloat16)
        for k in range(1, nt):
            back(k, s).start()
        own(s).start()
        return carry

    lax.fori_loop(0, span, attend_unit, 0)

    def drain(s, carry):
        own(s).wait()
        for k in range(1, nt):
            back(k, s).wait_recv()
            back(k, s).wait_send()
            forward(k, s).wait_send()
        return carry

    lax.fori_loop(0, span, drain, 0)
    for index, (dr, dc) in enumerate(STEPS):
        @pl.when(jnp.logical_and(inside(h + dr, nh), inside(w + dc, nw)))
        def _(index=index):
            halo(index, 1).wait_send()
    for side, step in ((0, -1), (1, 1)):
        @pl.when(inside(t + step, nt))
        def _(side=side):
            for s in range(span):
                edge(side, s, 1).wait_send()


def per_device(sizes, video, w_space, w_time, norm_gain, norm_bias, w_qkv, w_out):
    frames, rows, cols, channels = video.shape
    nt, nh, nw = sizes
    span = rows // nt
    unit = cols * frames
    total = nt * frames
    hbm = pl.BlockSpec(memory_space=pl.ANY)
    vmem = pl.BlockSpec(memory_space=pltpu.VMEM)
    bf16, f32, dma = jnp.bfloat16, jnp.float32, pltpu.SemaphoreType.DMA
    two = 2 if rows % 2 == 0 else 1
    pixels = rows * cols * frames
    lanes = math.gcd(channels, 128)
    halves = channels // lanes
    out = pl.pallas_call(
        functools.partial(kernel, sizes),
        out_shape=jax.ShapeDtypeStruct(video.shape, bf16),
        in_specs=[hbm] * 3 + [vmem] * 2 + [hbm] * 2,
        out_specs=hbm,
        scratch_shapes=[
            pltpu.VMEM(video.shape, bf16), pltpu.VMEM(w_space.shape, bf16), pltpu.VMEM(w_time.shape, bf16),
            pltpu.VMEM(w_qkv.shape, bf16), pltpu.VMEM(w_out.shape, bf16),
            pltpu.VMEM((rows + 2, cols + 2, frames, channels), bf16),
            pltpu.VMEM((rows, unit, channels), bf16),
            pltpu.VMEM((2, span, nt, cols, channels), bf16),
            pltpu.VMEM((2, span, nt, cols, channels), bf16),
            pltpu.VMEM((nt * halves, unit, lanes), f32),
            pltpu.VMEM((two * halves, unit, lanes), f32),
            pltpu.VMEM((halves, cols * total, lanes), f32),
            pltpu.VMEM((nt, span, unit, channels), bf16),
            pltpu.VMEM((nt, span, unit, channels), bf16),
            pltpu.VMEM((nt, span, frames, cols, channels), bf16),
            pltpu.VMEM((cols, total, 3 * channels), bf16),
            pltpu.VMEM((cols, total, channels), bf16),
            pltpu.VMEM((cols, total, channels), bf16),
            pltpu.VMEM((8, channels), f32),
            pltpu.VMEM((nt, 8, channels), f32),
            pltpu.VMEM((nh, 8, channels), f32),
            pltpu.VMEM((nw, 8, channels), f32),
            dma((5,)), dma((span,)), dma((len(STEPS),)), dma((len(STEPS),)), dma((2, span)), dma((2, span)),
            dma((nt, span)), dma((nt, span)), dma((nt, span)), dma((nt, span)),
            dma((nt,)), dma((nt,)), dma((nh,)), dma((nh,)), dma((nw,)), dma((nw,)),
        ],
        compiler_params=pltpu.CompilerParams(
            collective_id=0, has_side_effects=True, vmem_limit_bytes=60 * 1024 * 1024
        ),
        cost_estimate=pl.CostEstimate(
            flops=2 * pixels * channels * channels * 20,
            bytes_accessed=4 * pixels * channels, transcendentals=pixels * 64 * HEADS,
        ),
    )(
        video, w_space, w_time, norm_gain.reshape(1, channels), norm_bias.reshape(1, channels), w_qkv, w_out
    )
    return out


def solution(mesh):
    sizes = tuple(mesh.shape[name] for name in ("tm", "height", "width"))
    placed = (P("tm", "height", "width", None), P(), P(), P(), P(), P(), P())
    return jax.shard_map(
        functools.partial(per_device, sizes),
        mesh=mesh,
        in_specs=placed,
        out_specs=P("tm", "height", "width", None),
        check_vma=False,
    )
```
